512 devices in a mesh: blk: 64 (over y_hi, z, core), acc: 4 (over x), tail: 2 (over y_lo).
Axes of the slice: x: 4, y: 8 (y_hi: 4, y_lo: 2; y = y_hi * 2 + y_lo), z: 8, core: 2. Of those that a mesh axis runs over, the one named last changes fastest.
Arguments:
- reciprocal_spectra: float32 [4, 2, 64, 4096], P(None, None, 'acc'), may hold values from -6 to 6
- divisor: float32 [128, 131072], P(('blk', 'tail'), 'acc'), may hold values from -1 to 1
Outputs:
- middle_product: float32 [128, 131072], P(('blk', 'tail'), 'acc')
The draws below stay inside these ranges and needn't reach their ends.
All inputs are finite; a program needn't handle non-finite values.
Results may differ from the reference program's by a relative error of at most 0.0003.
Values sent between devices are 32-bit elements; how exact they have to be, the bound alone decides.
A program may use at most 64 MiB of HBM per device.

```python
import jax
import jax.numpy as jnp
from jax import lax

RADIX = 64
ROUNDS = 4
LIMBS = 131072
NBLOCKS = 128
STRIDE = 2


def steps_of(own_key, extent, split, smallest, largest):
    factor_of, own = 1.0, jax.random.fold_in(own_key, 6)
    for dim, parts in split:
        steps = jnp.exp(jax.random.uniform(jax.random.fold_in(own, dim), (parts,), jnp.float32, smallest / len(split), largest / len(split)))
        factor_of = factor_of * jnp.repeat(steps, extent[dim] // parts).reshape([-1 if axis == dim else 1 for axis in range(len(extent))])
    return factor_of


def centred(stream_key, extent, width, bound, pieces=(), held_as=jnp.bfloat16):
    result = jax.random.normal(stream_key, extent, jnp.float32) * width
    if len(pieces) > 0:
        result = steps_of(stream_key, extent, pieces, -0.22, 0.18) * result
    return jnp.clip(result, min=-bound, max=bound).astype(held_as)


def setup_inputs(seed: int = 0) -> dict:
    key_of = jax.random.split(jax.random.key(seed), 3)
    reciprocal_spectra = centred(key_of[0], (ROUNDS, 2, RADIX, RADIX * RADIX), 1.0, 6.0, ((2, 4),), jnp.float32)
    divisor = jnp.clip(jax.random.uniform(key_of[1], (NBLOCKS, LIMBS), jnp.float32, -1.0, 1.0) * steps_of(key_of[1], (NBLOCKS, LIMBS), ((0, 128), (1, 4)), -0.4, 0.0), -1.0, 1.0)
    return dict(reciprocal_spectra=reciprocal_spectra, divisor=divisor)


def reference(reciprocal_spectra, divisor):
    length = RADIX ** 3
    ordered = reciprocal_spectra.reshape(ROUNDS, 2, RADIX, RADIX, RADIX).transpose(0, 1, 4, 3, 2).reshape(ROUNDS, 2, length)
    recip_full = ordered[:, 0] + 1j * ordered[:, 1]
    divisor_spectra = jnp.fft.fft(divisor, n=length, axis=-1)

    def one_block(block_index):
        total = jnp.zeros((length,), divisor_spectra.dtype)
        for step_index in range(ROUNDS):
            source = (block_index - step_index * STRIDE) % NBLOCKS
            picked = lax.dynamic_index_in_dim(divisor_spectra, source, 0, keepdims=False)
            total = total + recip_full[step_index] * picked
        return jnp.real(jnp.fft.ifft(total)).astype(jnp.float32)

    block_products = lax.map(one_block, jnp.arange(NBLOCKS, dtype=jnp.int32))
    lower_part = block_products[:, :LIMBS]
    upper_part = block_products[:, LIMBS:]
    return (lower_part + jnp.roll(upper_part, 1, axis=0)).astype(jnp.float32)
```

```python
import functools

import jax
import jax.numpy as jnp
import ml_dtypes
import numpy as np
from jax import lax
from jax.experimental import pallas as pl
from jax.experimental.pallas import tpu as pltpu
from jax.sharding import PartitionSpec as P

LENGTH = 262144
ACC = 4
ROWS = 16
OUTER = 64
MID = 32
LANES = 128
QUARTER = 256
HALF = QUARTER // 2
CHUNK = 4
CHUNKS = ROWS // CHUNK
ROUNDS = 4


def high_low(table):
    high = table.astype(ml_dtypes.bfloat16)
    low = (table - high.astype(np.float64)).astype(ml_dtypes.bfloat16)
    return high, low


def stacked_left(table):
    high, low = high_low(table)
    return np.concatenate(
        [
            np.concatenate([high, high], axis=-1),
            np.concatenate([low, np.zeros_like(low)], axis=-1),
        ],
        axis=-2,
    )


def root(product, modulus):
    angle = (product % modulus) * (-2.0 * np.pi / modulus)
    return np.cos(angle), np.sin(angle)


@functools.lru_cache(maxsize=None)
def tables():
    rows = np.arange(OUTER)
    limb = np.arange(OUTER)
    mid = np.arange(MID)
    lane = np.arange(LANES)
    kappa = np.concatenate([np.arange(0, MID, 2), np.arange(1, MID, 2)])
    bins = 2 * (lane % 64) + lane // 64
    first, first_back = [], []
    for place in range(ACC):
        own = rows[place * ROWS : (place + 1) * ROWS]
        real, imag = root(own[:, None] * limb[None, :], OUTER)
        first.append(stacked_left(np.concatenate([real, imag], axis=0)))
        order = [(place + 2) % ACC, (place + 1) % ACC, (place + 3) % ACC, place]
        kept = np.concatenate([np.arange(8 * q, 8 * q + 8) for q in order])
        real, imag = root(kept[:, None] * own[None, :], OUTER)
        first_back.append(stacked_left(np.concatenate([real, imag], axis=1) / LENGTH))
    freq = rows[:, None] + OUTER * kappa[None, :]
    real, imag = root(freq[:, :, None] * mid[None, None, :], 2048)
    second = stacked_left(
        np.concatenate(
            [np.concatenate([real, -imag], axis=2), np.concatenate([imag, real], axis=2)], axis=1
        )
    )
    real, imag = real.transpose(0, 2, 1), -imag.transpose(0, 2, 1)
    second_back = stacked_left(
        np.concatenate(
            [np.concatenate([real, -imag], axis=2), np.concatenate([imag, real], axis=2)], axis=1
        )
    )
    real, imag = root(freq[:, :, None] * lane[None, None, :], LENGTH)
    twiddle = np.stack([real, imag], axis=1).astype(np.float32)
    real, imag = root(lane[:, None] * bins[None, :], LANES)
    third = np.stack(
        high_low(
            np.concatenate(
                [np.concatenate([real, imag], axis=1), np.concatenate([-imag, real], axis=1)], axis=0
            )
        )
    )
    real, imag = real.T, -imag.T
    third_back = np.stack(
        high_low(
            np.concatenate(
                [np.concatenate([real, imag], axis=1), np.concatenate([-imag, real], axis=1)], axis=0
            )
        )
    )
    return (
        np.stack(first),
        second,
        twiddle,
        third,
        third_back,
        second_back,
        np.stack(first_back),
    )


def split(value):
    high = value.astype(jnp.bfloat16)
    low = (value - high.astype(jnp.float32)).astype(jnp.bfloat16)
    return high, low


def dot(first, second):
    return jnp.dot(first, second, preferred_element_type=jnp.float32)


def left_product(stacked, value):
    high, low = split(value)
    both = dot(stacked, jnp.concatenate([high, low], axis=0))
    rows = both.shape[0] // 2
    return both[:rows] + both[rows:]


def right_product(value, table):
    high, low = split(value)
    rows = value.shape[0]
    both = dot(jnp.concatenate([high, low], axis=0), table[0])
    return both[:rows] + both[rows:] + dot(high, table[1])


def exchanged(value, lower):
    top, bottom = value[: MID // 2], value[MID // 2 :]
    return jnp.concatenate(
        [
            jnp.where(lower, top, pltpu.roll(bottom, 64, 1)),
            jnp.where(lower, pltpu.roll(top, 64, 1), bottom),
        ],
        axis=0,
    )


def kernel(
    blocks,
    recip_hbm,
    limbs_hbm,
    first_hbm,
    second_hbm,
    twiddle_hbm,
    third_ref,
    third_back_ref,
    second_back_hbm,
    first_back_hbm,
    out_ref,
    recip,
    limbs,
    first,
    second,
    twiddle,
    second_back,
    first_back,
    mixed,
    spectra,
    total,
    back,
    result,
    transit,
    arrived,
    local_sem,
    over_send,
    over_recv,
    gather_send,
    gather_recv,
    ring_send,
    ring_recv,
    sum_send,
    sum_recv,
):
    blk = lax.axis_index("blk")
    acc = lax.axis_index("acc")
    tail = lax.axis_index("tail")
    right = {"blk": blk, "acc": lax.rem(acc + 1, ACC), "tail": tail}
    left = {"blk": blk, "acc": lax.rem(acc + ACC - 1, ACC), "tail": tail}
    later = {"blk": lax.rem(blk + tail, blocks), "acc": acc, "tail": 1 - tail}
    earlier = {"blk": lax.rem(blk + blocks - 1 + tail, blocks), "acc": acc, "tail": 1 - tail}
    onward = {"blk": lax.rem(blk + 1, blocks), "acc": acc, "tail": tail}
    backward = {"blk": lax.rem(blk + blocks - 1, blocks), "acc": acc, "tail": tail}

    def remote(src, dst, send_sem, recv_sem, device):
        return pltpu.make_async_remote_copy(
            src_ref=src,
            dst_ref=dst,
            send_sem=send_sem,
            recv_sem=recv_sem,
            device_id=device,
            device_id_type=pl.DeviceIdType.MESH,
        )

    def quarter(part, owner, start, size):
        first_row = pl.multiple_of((part * ACC + owner) * QUARTER + start, HALF)
        return limbs.at[pl.ds(first_row, size)]

    barrier = pltpu.get_barrier_semaphore()
    for device in (right, left, later, earlier, onward, backward):
        pl.semaphore_signal(barrier, inc=1, device_id=device, device_id_type=pl.DeviceIdType.MESH)
    own_rows = pl.ds(acc * ROWS, ROWS)
    own_limbs = pltpu.make_async_copy(limbs_hbm, quarter(0, acc, 0, QUARTER), local_sem.at[0])
    local = [
        pltpu.make_async_copy(first_hbm.at[acc], first, local_sem.at[1]),
        pltpu.make_async_copy(second_hbm.at[own_rows], second, local_sem.at[2]),
        pltpu.make_async_copy(twiddle_hbm.at[own_rows], twiddle, local_sem.at[3]),
        pltpu.make_async_copy(second_back_hbm.at[own_rows], second_back, local_sem.at[4]),
        pltpu.make_async_copy(first_back_hbm.at[acc], first_back, local_sem.at[5]),
        pltpu.make_async_copy(recip_hbm, recip, local_sem.at[6]),
    ]
    own_limbs.start()
    for copy in local:
        copy.start()
    own_limbs.wait()
    pl.semaphore_wait(barrier, 6)

    over = remote(
        quarter(0, acc, 0, QUARTER),
        quarter(1, acc, 0, QUARTER),
        over_send.at[0],
        over_recv.at[0],
        later,
    )
    over.start()

    def gather(part, step, owner, start, device):
        ref = quarter(part, owner, start, HALF)
        return remote(ref, ref, gather_send.at[part, step], gather_recv.at[part, step], device)

    from_left = lax.rem(acc + ACC - 1, ACC)
    from_right = lax.rem(acc + 1, ACC)
    copies = []

    def spread(part):
        steps = [
            gather(part, 0, acc, 0, right),
            gather(part, 1, acc, HALF, left),
            gather(part, 2, acc, HALF, right),
            gather(part, 3, acc, 0, left),
        ]
        for copy in steps:
            copy.start()
        return steps

    def pass_on(part, steps):
        steps[0].wait_recv()
        to_right = gather(part, 4, from_left, 0, right)
        to_right.start()
        steps[1].wait_recv()
        to_left = gather(part, 5, from_right, HALF, left)
        to_left.start()
        return [to_right, to_left]

    own_steps = spread(0)
    over.wait_recv()
    earlier_steps = spread(1)
    own_steps += pass_on(0, own_steps)
    earlier_steps += pass_on(1, earlier_steps)
    for copy in own_steps[2:] + earlier_steps[2:]:
        copy.wait_recv()
    for copy in local:
        copy.wait()

    lower = lax.broadcasted_iota(jnp.int32, (MID // 2, LANES), 1) < 64

    def first_step(pair, carry):
        values = [limbs[pl.ds(2 * pair + side, OUTER, stride=MID)] for side in range(2)]
        product = left_product(first[...], jnp.concatenate(values, axis=1))
        for side in range(2):
            start = pl.multiple_of((2 * pair + side) * 2 * ROWS, 2 * ROWS)
            mixed[pl.ds(start, 2 * ROWS)] = product[:, side * LANES : (side + 1) * LANES]
        return carry

    lax.fori_loop(0, MID // 2, first_step, 0)

    def ring(step, chunk):
        rows = pl.ds(chunk * CHUNK, CHUNK)
        return remote(
            spectra.at[step, rows],
            spectra.at[step + 1, rows],
            ring_send.at[step, chunk],
            ring_recv.at[step, chunk],
            onward,
        )

    def forward(chunk, carry):
        reals, imags = [], []
        for place in range(CHUNK):
            row = chunk * CHUNK + place
            value = jnp.concatenate(
                [
                    mixed[pl.ds(row, MID, stride=2 * ROWS)],
                    mixed[pl.ds(ROWS + row, MID, stride=2 * ROWS)],
                ],
                axis=0,
            )
            product = left_product(second[row], value)
            real, imag = product[:MID], product[MID:]
            turn_real, turn_imag = twiddle[row, 0], twiddle[row, 1]
            reals.append(real * turn_real - imag * turn_imag)
            imags.append(real * turn_imag + imag * turn_real)
        value = jnp.concatenate(
            [jnp.concatenate(reals, axis=0), jnp.concatenate(imags, axis=0)], axis=1
        )
        product = right_product(value, third_ref)
        for place in range(CHUNK):
            rows = product[place * MID : (place + 1) * MID]
            spectra[0, chunk * CHUNK + place, 0] = exchanged(rows[:, :LANES], lower)
            spectra[0, chunk * CHUNK + place, 1] = exchanged(rows[:, LANES:], lower)
        ring(0, chunk).start()
        return carry

    lax.fori_loop(0, CHUNKS, forward, 0)

    def term(step, row, chunk, place):
        start = step * 1024 + (chunk // 2) * 256 + lax.rem(chunk, 2) * CHUNK + place
        recip_real = recip[pl.ds(start, MID, stride=8)]
        recip_imag = recip[pl.ds(start + 512, MID, stride=8)]
        real, imag = spectra[step, row, 0], spectra[step, row, 1]
        return recip_real * real - recip_imag * imag, recip_real * imag + recip_imag * real

    def arrive_first(chunk, carry):
        ring(0, chunk).wait_recv()
        ring(1, chunk).start()
        for place in range(CHUNK):
            row = chunk * CHUNK + place
            real, imag = term(0, row, chunk, place)
            more_real, more_imag = term(1, row, chunk, place)
            total[row, 0] = real + more_real
            total[row, 1] = imag + more_imag
        return carry

    lax.fori_loop(0, CHUNKS, arrive_first, 0)

    def arrive_second(chunk, carry):
        ring(1, chunk).wait_recv()
        ring(2, chunk).start()
        for place in range(CHUNK):
            row = chunk * CHUNK + place
            real, imag = term(2, row, chunk, place)
            total[row, 0] += real
            total[row, 1] += imag
        return carry

    lax.fori_loop(0, CHUNKS, arrive_second, 0)

    def arrive_third(chunk, carry):
        ring(2, chunk).wait_recv()
        reals, imags = [], []
        for place in range(CHUNK):
            row = chunk * CHUNK + place
            real, imag = term(3, row, chunk, place)
            reals.append(exchanged(total[row, 0] + real, lower))
            imags.append(exchanged(total[row, 1] + imag, lower))
        value = jnp.concatenate(
            [jnp.concatenate(reals, axis=0), jnp.concatenate(imags, axis=0)], axis=1
        )
        product = right_product(value, third_back_ref)
        for place in range(CHUNK):
            row = chunk * CHUNK + place
            real = product[place * MID : (place + 1) * MID, :LANES]
            imag = product[place * MID : (place + 1) * MID, LANES:]
            turn_real, turn_imag = twiddle[row, 0], twiddle[row, 1]
            turned = jnp.concatenate(
                [real * turn_real + imag * turn_imag, imag * turn_real - real * turn_imag], axis=0
            )
            unmixed = left_product(second_back[row], turned)
            back[pl.ds(row, MID, stride=2 * ROWS)] = unmixed[:MID]
            back[pl.ds(ROWS + row, MID, stride=2 * ROWS)] = unmixed[MID:]
        return carry

    lax.fori_loop(0, CHUNKS, arrive_third, 0)

    def last_step(pair, carry):
        values = []
        for side in range(2):
            start = pl.multiple_of((2 * pair + side) * 2 * ROWS, 2 * ROWS)
            values.append(back[pl.ds(start, 2 * ROWS)])
        product = left_product(first_back[...], jnp.concatenate(values, axis=1))
        for side in range(2):
            result[pl.ds(2 * pair + side, MID, stride=MID)] = product[
                :, side * LANES : (side + 1) * LANES
            ]
        return carry

    lax.fori_loop(0, MID // 2, last_step, 0)

    def part(place, start):
        return result.at[pl.ds(place * QUARTER + start, HALF)]

    to_right = remote(part(0, 0), transit.at[0], sum_send.at[0], sum_recv.at[0], right)
    to_left = remote(part(0, HALF), transit.at[1], sum_send.at[1], sum_recv.at[1], left)
    plain_right = remote(part(1, HALF), arrived.at[0], sum_send.at[2], sum_recv.at[2], right)
    plain_left = remote(part(2, 0), arrived.at[1], sum_send.at[3], sum_recv.at[3], left)
    summed_right = remote(part(1, 0), arrived.at[2], sum_send.at[4], sum_recv.at[4], right)
    summed_left = remote(part(2, HALF), arrived.at[3], sum_send.at[5], sum_recv.at[5], left)
    to_right.start()
    to_left.start()
    plain_right.start()
    plain_left.start()
    to_right.wait_recv()
    result[QUARTER : QUARTER + HALF] += transit[0]
    summed_right.start()
    to_left.wait_recv()
    result[2 * QUARTER + HALF : 3 * QUARTER] += transit[1]
    summed_left.start()
    plain_right.wait_recv()
    plain_left.wait_recv()
    summed_right.wait_recv()
    out_ref[:HALF] = result[3 * QUARTER : 3 * QUARTER + HALF] + arrived[1] + arrived[2]
    summed_left.wait_recv()
    out_ref[HALF:] = result[3 * QUARTER + HALF :] + arrived[0] + arrived[3]

    sent = [over, *own_steps, *earlier_steps]
    sent += [to_right, to_left, plain_right, plain_left, summed_right, summed_left]
    for copy in sent:
        copy.wait_send()

    def drain(chunk, carry):
        for step in range(ROUNDS - 1):
            ring(step, chunk).wait_send()
        return carry

    lax.fori_loop(0, CHUNKS, drain, 0)


def per_device(blocks, reciprocal_spectra, divisor):
    recip = reciprocal_spectra.reshape(ROUNDS, 2, 2, 8, MID, LANES)
    recip = recip.transpose(0, 1, 2, 4, 3, 5).reshape(ROUNDS * 1024, LANES)
    limbs = divisor.reshape(QUARTER, LANES)
    constants = [jnp.asarray(table) for table in tables()]
    first, second, twiddle, third, third_back, second_back, first_back = constants
    anywhere = pl.BlockSpec(memory_space=pl.ANY)
    vmem = pl.BlockSpec(memory_space=pltpu.VMEM)
    out = pl.pallas_call(
        functools.partial(kernel, blocks),
        out_shape=jax.ShapeDtypeStruct((QUARTER, LANES), jnp.float32),
        in_specs=[anywhere] * 5 + [vmem] * 2 + [anywhere] * 2,
        out_specs=vmem,
        scratch_shapes=[
            pltpu.VMEM((ROUNDS * 1024, LANES), jnp.float32),
            pltpu.VMEM((2 * ACC * QUARTER, LANES), jnp.float32),
            pltpu.VMEM(first.shape[1:], jnp.bfloat16),
            pltpu.VMEM((ROWS, *second.shape[1:]), jnp.bfloat16),
            pltpu.VMEM((ROWS, *twiddle.shape[1:]), jnp.float32),
            pltpu.VMEM((ROWS, *second_back.shape[1:]), jnp.bfloat16),
            pltpu.VMEM(first_back.shape[1:], jnp.bfloat16),
            pltpu.VMEM((MID * 2 * ROWS, LANES), jnp.float32),
            pltpu.VMEM((ROUNDS, ROWS, 2, MID, LANES), jnp.float32),
            pltpu.VMEM((ROWS, 2, MID, LANES), jnp.float32),
            pltpu.VMEM((MID * 2 * ROWS, LANES), jnp.float32),
            pltpu.VMEM((ACC * QUARTER, LANES), jnp.float32),
            pltpu.VMEM((2, HALF, LANES), jnp.float32),
            pltpu.VMEM((4, HALF, LANES), jnp.float32),
            pltpu.SemaphoreType.DMA((7,)),
            pltpu.SemaphoreType.DMA((1,)),
            pltpu.SemaphoreType.DMA((1,)),
            pltpu.SemaphoreType.DMA((2, 6)),
            pltpu.SemaphoreType.DMA((2, 6)),
            pltpu.SemaphoreType.DMA((ROUNDS - 1, CHUNKS)),
            pltpu.SemaphoreType.DMA((ROUNDS - 1, CHUNKS)),
            pltpu.SemaphoreType.DMA((6,)),
            pltpu.SemaphoreType.DMA((6,)),
        ],
        compiler_params=pltpu.CompilerParams(
            collective_id=0, has_side_effects=True, vmem_limit_bytes=60 * 1024 * 1024
        ),
    )(recip, limbs, first, second, twiddle, third, third_back, second_back, first_back)
    return out.reshape(1, QUARTER * LANES)


def solution(mesh):
    in_specs = (P(None, None, "acc", None), P(("blk", "tail"), "acc"))
    out_specs = P(("blk", "tail"), "acc")
    return jax.shard_map(
        functools.partial(per_device, mesh.shape["blk"]),
        mesh=mesh,
        in_specs=in_specs,
        out_specs=out_specs,
        check_vma=False,
    )
```

```python
import functools

import jax
import jax.numpy as jnp
import ml_dtypes
import numpy as np
from jax import lax
from jax.experimental import pallas as pl
from jax.experimental.pallas import tpu as pltpu
from jax.sharding import PartitionSpec as P

LENGTH = 262144
ACC = 4
OWNED = 16
ROWS = 9
PADDED = 32
OUTER = 64
MID = 32
LANES = 128
QUARTER = 256
HALF = QUARTER // 2
CHUNK = 3
CHUNKS = ROWS // CHUNK
ROUNDS = 4
CORES = 2
CYCLE = 16


def high_low(table):
    high = table.astype(ml_dtypes.bfloat16)
    low = (table - high.astype(np.float64)).astype(ml_dtypes.bfloat16)
    return high, low


def stacked_left(table):
    high, low = high_low(table)
    return np.concatenate(
        [
            np.concatenate([high, high], axis=-1),
            np.concatenate([low, np.zeros_like(low)], axis=-1),
        ],
        axis=-2,
    )


def root(product, modulus):
    angle = (product % modulus) * (-2.0 * np.pi / modulus)
    return np.cos(angle), np.sin(angle)


@functools.lru_cache(maxsize=None)
def tables():
    rows = np.arange(OUTER)
    limb = np.arange(OUTER)
    mid = np.arange(MID)
    lane = np.arange(LANES)
    kappa = np.concatenate([np.arange(0, MID, 2), np.arange(1, MID, 2)])
    bins = 2 * (lane % 64) + lane // 64
    first, first_back = [], []
    for place in range(ACC):
        own = rows[place * OWNED : place * OWNED + ROWS]
        real, imag = root(own[:, None] * limb[None, :], OUTER)
        empty = np.zeros((PADDED - 2 * ROWS, OUTER))
        first.append(stacked_left(np.concatenate([real, imag, empty], axis=0)))
        order = [(place + 2) % ACC, (place + 1) % ACC, (place + 3) % ACC, place]
        kept = np.concatenate([np.arange(8 * q, 8 * q + 8) for q in order])
        real, imag = root(kept[:, None] * own[None, :], OUTER)
        empty = np.zeros((len(kept), PADDED - 2 * ROWS))
        first_back.append(stacked_left(np.concatenate([real, imag, empty], axis=1) / LENGTH))
    freq = rows[:, None] + OUTER * kappa[None, :]
    real, imag = root(freq[:, :, None] * mid[None, None, :], 2048)
    second = stacked_left(
        np.concatenate(
            [np.concatenate([real, -imag], axis=2), np.concatenate([imag, real], axis=2)], axis=1
        )
    )
    real, imag = real.transpose(0, 2, 1), -imag.transpose(0, 2, 1)
    second_back = stacked_left(
        np.concatenate(
            [np.concatenate([real, -imag], axis=2), np.concatenate([imag, real], axis=2)], axis=1
        )
    )
    real, imag = root(freq[:, :, None] * lane[None, None, :], LENGTH)
    twiddle = np.stack([real, imag], axis=1).astype(np.float32)
    real, imag = root(lane[:, None] * bins[None, :], LANES)
    third = np.stack(
        high_low(
            np.concatenate(
                [np.concatenate([real, imag], axis=1), np.concatenate([-imag, real], axis=1)], axis=0
            )
        )
    )
    real, imag = real.T, -imag.T
    third_back = np.stack(
        high_low(
            np.concatenate(
                [np.concatenate([real, imag], axis=1), np.concatenate([-imag, real], axis=1)], axis=0
            )
        )
    )
    return (
        np.stack(first),
        second,
        twiddle,
        third,
        third_back,
        second_back,
        np.stack(first_back),
        np.concatenate([np.eye(LANES)[::-1]] * 2, axis=0).astype(ml_dtypes.bfloat16),
    )


def split(value):
    high = value.astype(jnp.bfloat16)
    low = (value - high.astype(jnp.float32)).astype(jnp.bfloat16)
    return high, low


def dot(first, second):
    return jnp.dot(first, second, preferred_element_type=jnp.float32)


def left_product(stacked, value):
    high, low = split(value)
    both = dot(stacked, jnp.concatenate([high, low], axis=0))
    rows = both.shape[0] // 2
    return both[:rows] + both[rows:]


def right_product(value, table):
    high, low = split(value)
    rows = value.shape[0]
    both = dot(jnp.concatenate([high, low], axis=0), table[0])
    return both[:rows] + both[rows:] + dot(high, table[1])


def exchanged(value, lower):
    top, bottom = value[: MID // 2], value[MID // 2 :]
    return jnp.concatenate(
        [
            jnp.where(lower, top, pltpu.roll(bottom, 64, 1)),
            jnp.where(lower, pltpu.roll(top, 64, 1), bottom),
        ],
        axis=0,
    )


def kernel(
    blocks,
    recip_hbm,
    limbs_hbm,
    first_hbm,
    second_hbm,
    twiddle_hbm,
    third_ref,
    third_back_ref,
    flip_ref,
    second_back_hbm,
    first_back_hbm,
    out_ref,
    recip,
    paired,
    flipped,
    weights,
    limbs,
    first,
    second,
    twiddle,
    second_back,
    first_back,
    mixed,
    spectra,
    back,
    result,
    transit,
    arrived,
    local_sem,
    over_send,
    over_recv,
    gather_send,
    gather_recv,
    share_send,
    share_recv,
    ring_send,
    ring_recv,
    sum_send,
    sum_recv,
):
    blk = lax.axis_index("blk")
    acc = lax.axis_index("acc")
    tail = lax.axis_index("tail")
    right = {"blk": blk, "acc": lax.rem(acc + 1, ACC), "tail": tail}
    left = {"blk": blk, "acc": lax.rem(acc + ACC - 1, ACC), "tail": tail}
    later = {"blk": lax.rem(blk + tail, blocks), "acc": acc, "tail": 1 - tail}
    earlier = {"blk": lax.rem(blk + blocks - 1 + tail, blocks), "acc": acc, "tail": 1 - tail}
    onward = {"blk": lax.rem(blk + 1, blocks), "acc": acc, "tail": tail}
    backward = {"blk": lax.rem(blk + blocks - 1, blocks), "acc": acc, "tail": tail}
    partner = {"blk": blk, "acc": ACC - 1 - acc, "tail": tail}
    cycle = min(CYCLE, blocks)
    spot = lax.rem(blk, cycle)
    core = lax.rem(blk, CORES)
    parity = lax.rem(spot // CORES, 2)
    mate = {"blk": blk + 1 - 2 * core, "acc": acc, "tail": tail}
    below = {"blk": blk - spot + lax.rem(spot + cycle - CORES, cycle), "acc": acc, "tail": tail}
    above = {"blk": blk - spot + lax.rem(spot + CORES, cycle), "acc": acc, "tail": tail}

    def remote(src, dst, send_sem, recv_sem, device):
        return pltpu.make_async_remote_copy(
            src_ref=src,
            dst_ref=dst,
            send_sem=send_sem,
            recv_sem=recv_sem,
            device_id=device,
            device_id_type=pl.DeviceIdType.MESH,
        )

    def quarter(part, owner, start, size):
        first_row = pl.multiple_of((part * ACC + owner) * QUARTER + start, HALF)
        return limbs.at[pl.ds(first_row, size)]

    barrier = pltpu.get_barrier_semaphore()
    for device in (right, left, later, earlier, onward, backward, below, above):
        pl.semaphore_signal(barrier, inc=1, device_id=device, device_id_type=pl.DeviceIdType.MESH)
    own_rows = pl.ds(acc * OWNED, ROWS)
    own_limbs = pltpu.make_async_copy(limbs_hbm, quarter(0, acc, 0, QUARTER), local_sem.at[0])
    local = [
        pltpu.make_async_copy(first_hbm.at[acc], first, local_sem.at[1]),
        pltpu.make_async_copy(second_hbm.at[own_rows], second, local_sem.at[2]),
        pltpu.make_async_copy(twiddle_hbm.at[own_rows], twiddle, local_sem.at[3]),
        pltpu.make_async_copy(second_back_hbm.at[own_rows], second_back, local_sem.at[4]),
        pltpu.make_async_copy(first_back_hbm.at[acc], first_back, local_sem.at[5]),
        pltpu.make_async_copy(recip_hbm, recip, local_sem.at[6]),
    ]
    own_limbs.start()
    for copy in local:
        copy.start()
    own_limbs.wait()

    def clear(mid, carry):
        start = pl.multiple_of(mid * PADDED, PADDED)
        back[pl.ds(start + 16, PADDED - 16)] = jnp.zeros((PADDED - 16, LANES), jnp.float32)
        return carry

    lax.fori_loop(0, MID, clear, 0)
    pl.semaphore_wait(barrier, 8)

    over = remote(
        quarter(0, acc, 0, QUARTER),
        quarter(1, acc, 0, QUARTER),
        over_send.at[0],
        over_recv.at[0],
        later,
    )
    over.start()

    def gather(part, step, owner, start, device):
        ref = quarter(part, owner, start, HALF)
        return remote(ref, ref, gather_send.at[part, step], gather_recv.at[part, step], device)

    from_left = lax.rem(acc + ACC - 1, ACC)
    from_right = lax.rem(acc + 1, ACC)

    def spread(part):
        steps = [
            gather(part, 0, acc, 0, right),
            gather(part, 1, acc, HALF, left),
            gather(part, 2, acc, HALF, right),
            gather(part, 3, acc, 0, left),
        ]
        for copy in steps:
            copy.start()
        return steps

    def pass_on(part, steps):
        steps[0].wait_recv()
        to_right = gather(part, 4, from_left, 0, right)
        to_right.start()
        steps[1].wait_recv()
        to_left = gather(part, 5, from_right, HALF, left)
        to_left.start()
        return [to_right, to_left]

    own_steps = spread(0)
    over.wait_recv()
    earlier_steps = spread(1)
    own_steps += pass_on(0, own_steps)
    earlier_steps += pass_on(1, earlier_steps)

    def share(step, source, round_index, device):
        found = []
        for side in range(2):
            start = pl.multiple_of(round_index * 1024 + side * 512 + 256, 256)
            slot = paired.at[round_index, side]
            found.append(
                remote(
                    recip_hbm.at[pl.ds(start, 256)] if source is None else slot,
                    slot,
                    share_send.at[step, side],
                    share_recv.at[step, side],
                    device,
                )
            )
        return found

    own_round = parity * 2 + core
    fetched = share(0, None, own_round, partner)
    to_mate = share(1, paired, own_round, mate)
    to_below = share(2, paired, own_round, below)
    relayed = share(3, paired, (1 - parity) * 2 + core, mate)
    for copy in fetched:
        copy.start()
    for copy in own_steps[2:] + earlier_steps[2:]:
        copy.wait_recv()
    for copy in local:
        copy.wait()

    lower = lax.broadcasted_iota(jnp.int32, (MID // 2, LANES), 1) < 64

    def first_step(pair, carry):
        values = [limbs[pl.ds(2 * pair + side, OUTER, stride=MID)] for side in range(2)]
        product = left_product(first[...], jnp.concatenate(values, axis=1))
        for side in range(2):
            start = pl.multiple_of((2 * pair + side) * PADDED, PADDED)
            mixed[pl.ds(start, PADDED)] = product[:, side * LANES : (side + 1) * LANES]
        return carry

    lax.fori_loop(0, MID // 2, first_step, 0)

    def ring(step, chunk):
        rows = pl.ds(chunk * CHUNK, CHUNK)
        return [
            remote(
                spectra.at[step, side, rows],
                spectra.at[step + 1, side, rows],
                ring_send.at[step, chunk, side],
                ring_recv.at[step, chunk, side],
                onward,
            )
            for side in range(2)
        ]

    def forward(chunk, carry):
        reals, imags = [], []
        for place in range(CHUNK):
            row = chunk * CHUNK + place
            value = jnp.concatenate(
                [
                    mixed[pl.ds(row, MID, stride=PADDED)],
                    mixed[pl.ds(ROWS + row, MID, stride=PADDED)],
                ],
                axis=0,
            )
            product = left_product(second[row], value)
            real, imag = product[:MID], product[MID:]
            turn_real, turn_imag = twiddle[row, 0], twiddle[row, 1]
            reals.append(real * turn_real - imag * turn_imag)
            imags.append(real * turn_imag + imag * turn_real)
        value = jnp.concatenate(
            [jnp.concatenate(reals, axis=0), jnp.concatenate(imags, axis=0)], axis=1
        )
        product = right_product(value, third_ref)
        for place in range(CHUNK):
            rows = product[place * MID : (place + 1) * MID]
            spectra[0, 0, chunk * CHUNK + place] = exchanged(rows[:, :LANES], lower)
            spectra[0, 1, chunk * CHUNK + place] = exchanged(rows[:, LANES:], lower)
        for copy in ring(0, chunk):
            copy.start()
        return carry

    lax.fori_loop(0, CHUNKS, forward, 0)

    for side in range(2):
        fetched[side].wait_recv()
        to_mate[side].start()
        to_below[side].start()

    def pass_ring(step):
        def body(chunk, carry):
            for come, go in zip(ring(step, chunk), ring(step + 1, chunk)):
                come.wait_recv()
                go.start()
            return carry

        lax.fori_loop(0, CHUNKS, body, 0)

    pass_ring(0)
    for side in range(2):
        to_below[side].wait_recv()
        relayed[side].start()
    pass_ring(1)
    for side in range(2):
        to_mate[side].wait_recv()
        relayed[side].wait_recv()

    def weigh(step, carry):
        for side in range(2):
            high, low = split(paired[step, side])
            turned = dot(jnp.concatenate([high, low], axis=1), flip_ref[...])
            for group in range(MID):
                flipped[side, pl.ds((MID - 1 - group) * 8, 8)] = turned[group * 8 : group * 8 + 8]
            start = step * 1024 + side * 512
            weights[step, side, 0] = recip[pl.ds(start, MID, stride=8)]
            weights[step, side, ROWS - 1] = recip[pl.ds(start + 256, MID, stride=8)]
            for row in range(1, ROWS - 1):
                own = recip[pl.ds(start + row, MID, stride=8)]
                other = flipped[side, pl.ds(8 - row, MID, stride=8)]
                weights[step, side, row] = own + other if side == 0 else own - other
        return carry

    lax.fori_loop(0, ROUNDS, weigh, 0)

    def arrive(chunk, carry):
        for copy in ring(2, chunk):
            copy.wait_recv()
        reals, imags = [], []
        for place in range(CHUNK):
            row = chunk * CHUNK + place
            total_real = total_imag = None
            for step in range(ROUNDS):
                weight_real, weight_imag = weights[step, 0, row], weights[step, 1, row]
                real, imag = spectra[step, 0, row], spectra[step, 1, row]
                term_real = weight_real * real - weight_imag * imag
                term_imag = weight_real * imag + weight_imag * real
                total_real = term_real if step == 0 else total_real + term_real
                total_imag = term_imag if step == 0 else total_imag + term_imag
            reals.append(exchanged(total_real, lower))
            imags.append(exchanged(total_imag, lower))
        value = jnp.concatenate(
            [jnp.concatenate(reals, axis=0), jnp.concatenate(imags, axis=0)], axis=1
        )
        product = right_product(value, third_back_ref)
        for place in range(CHUNK):
            row = chunk * CHUNK + place
            real = product[place * MID : (place + 1) * MID, :LANES]
            imag = product[place * MID : (place + 1) * MID, LANES:]
            turn_real, turn_imag = twiddle[row, 0], twiddle[row, 1]
            turned = jnp.concatenate(
                [real * turn_real + imag * turn_imag, imag * turn_real - real * turn_imag], axis=0
            )
            unmixed = left_product(second_back[row], turned)
            back[pl.ds(row, MID, stride=PADDED)] = unmixed[:MID]
            back[pl.ds(ROWS + row, MID, stride=PADDED)] = unmixed[MID:]
        return carry

    lax.fori_loop(0, CHUNKS, arrive, 0)

    def last_step(pair, carry):
        values = []
        for side in range(2):
            start = pl.multiple_of((2 * pair + side) * PADDED, PADDED)
            values.append(back[pl.ds(start, PADDED)])
        product = left_product(first_back[...], jnp.concatenate(values, axis=1))
        for side in range(2):
            result[pl.ds(2 * pair + side, MID, stride=MID)] = product[
                :, side * LANES : (side + 1) * LANES
            ]
        return carry

    lax.fori_loop(0, MID // 2, last_step, 0)

    def part(place, start):
        return result.at[pl.ds(place * QUARTER + start, HALF)]

    to_right = remote(part(0, 0), transit.at[0], sum_send.at[0], sum_recv.at[0], right)
    to_left = remote(part(0, HALF), transit.at[1], sum_send.at[1], sum_recv.at[1], left)
    plain_right = remote(part(1, HALF), arrived.at[0], sum_send.at[2], sum_recv.at[2], right)
    plain_left = remote(part(2, 0), arrived.at[1], sum_send.at[3], sum_recv.at[3], left)
    summed_right = remote(part(1, 0), arrived.at[2], sum_send.at[4], sum_recv.at[4], right)
    summed_left = remote(part(2, HALF), arrived.at[3], sum_send.at[5], sum_recv.at[5], left)
    to_right.start()
    to_left.start()
    plain_right.start()
    plain_left.start()
    to_right.wait_recv()
    result[QUARTER : QUARTER + HALF] += transit[0]
    summed_right.start()
    to_left.wait_recv()
    result[2 * QUARTER + HALF : 3 * QUARTER] += transit[1]
    summed_left.start()
    plain_right.wait_recv()
    plain_left.wait_recv()
    summed_right.wait_recv()
    out_ref[:HALF] = result[3 * QUARTER : 3 * QUARTER + HALF] + arrived[1] + arrived[2]
    summed_left.wait_recv()
    out_ref[HALF:] = result[3 * QUARTER + HALF :] + arrived[0] + arrived[3]

    sent = [over, *own_steps, *earlier_steps]
    sent += [*fetched, *to_mate, *to_below, *relayed]
    sent += [to_right, to_left, plain_right, plain_left, summed_right, summed_left]
    for copy in sent:
        copy.wait_send()

    def drain(chunk, carry):
        for step in range(ROUNDS - 1):
            for copy in ring(step, chunk):
                copy.wait_send()
        return carry

    lax.fori_loop(0, CHUNKS, drain, 0)


def per_device(blocks, reciprocal_spectra, divisor):
    recip = reciprocal_spectra.reshape(ROUNDS, 2, 2, 8, MID, LANES)
    recip = recip.transpose(0, 1, 2, 4, 3, 5).reshape(ROUNDS * 1024, LANES)
    limbs = divisor.reshape(QUARTER, LANES)
    constants = [jnp.asarray(table) for table in tables()]
    first, second, twiddle, third, third_back, second_back, first_back, flip = constants
    anywhere = pl.BlockSpec(memory_space=pl.ANY)
    vmem = pl.BlockSpec(memory_space=pltpu.VMEM)
    out = pl.pallas_call(
        functools.partial(kernel, blocks),
        out_shape=jax.ShapeDtypeStruct((QUARTER, LANES), jnp.float32),
        in_specs=[anywhere] * 5 + [vmem] * 3 + [anywhere] * 2,
        out_specs=vmem,
        scratch_shapes=[
            pltpu.VMEM((ROUNDS * 1024, LANES), jnp.float32),
            pltpu.VMEM((ROUNDS, 2, QUARTER, LANES), jnp.float32),
            pltpu.VMEM((2, QUARTER, LANES), jnp.float32),
            pltpu.VMEM((ROUNDS, 2, ROWS, MID, LANES), jnp.float32),
            pltpu.VMEM((2 * ACC * QUARTER, LANES), jnp.float32),
            pltpu.VMEM(first.shape[1:], jnp.bfloat16),
            pltpu.VMEM((ROWS, *second.shape[1:]), jnp.bfloat16),
            pltpu.VMEM((ROWS, *twiddle.shape[1:]), jnp.float32),
            pltpu.VMEM((ROWS, *second_back.shape[1:]), jnp.bfloat16),
            pltpu.VMEM(first_back.shape[1:], jnp.bfloat16),
            pltpu.VMEM((MID * PADDED, LANES), jnp.float32),
            pltpu.VMEM((ROUNDS, 2, ROWS, MID, LANES), jnp.float32),
            pltpu.VMEM((MID * PADDED, LANES), jnp.float32),
            pltpu.VMEM((ACC * QUARTER, LANES), jnp.float32),
            pltpu.VMEM((2, HALF, LANES), jnp.float32),
            pltpu.VMEM((4, HALF, LANES), jnp.float32),
            pltpu.SemaphoreType.DMA((7,)),
            pltpu.SemaphoreType.DMA((1,)),
            pltpu.SemaphoreType.DMA((1,)),
            pltpu.SemaphoreType.DMA((2, 6)),
            pltpu.SemaphoreType.DMA((2, 6)),
            pltpu.SemaphoreType.DMA((4, 2)),
            pltpu.SemaphoreType.DMA((4, 2)),
            pltpu.SemaphoreType.DMA((ROUNDS - 1, CHUNKS, 2)),
            pltpu.SemaphoreType.DMA((ROUNDS - 1, CHUNKS, 2)),
            pltpu.SemaphoreType.DMA((6,)),
            pltpu.SemaphoreType.DMA((6,)),
        ],
        compiler_params=pltpu.CompilerParams(
            collective_id=0, has_side_effects=True, vmem_limit_bytes=60 * 1024 * 1024
        ),
    )(recip, limbs, first, second, twiddle, third, third_back, flip, second_back, first_back)
    return out.reshape(1, QUARTER * LANES)


def solution(mesh):
    in_specs = (P(None, None, "acc", None), P(("blk", "tail"), "acc"))
    out_specs = P(("blk", "tail"), "acc")
    return jax.shard_map(
        functools.partial(per_device, mesh.shape["blk"]),
        mesh=mesh,
        in_specs=in_specs,
        out_specs=out_specs,
        check_vma=False,
    )
```

```python
import functools

import jax
import jax.numpy as jnp
import ml_dtypes
import numpy as np
from jax import lax
from jax.experimental import pallas as pl
from jax.experimental.pallas import tpu as pltpu
from jax.sharding import PartitionSpec as P

LENGTH = 262144
ACC = 4
OWNED = 16
ROWS = 9
PADDED = 32
OUTER = 64
MID = 32
LANES = 128
QUARTER = 256
HALF = QUARTER // 2
CHUNK = 3
CHUNKS = ROWS // CHUNK
ROUNDS = 4
CORES = 2
GROUP = 8
CYCLE = 16


def high_low(table):
    high = table.astype(ml_dtypes.bfloat16)
    low = (table - high.astype(np.float64)).astype(ml_dtypes.bfloat16)
    return high, low


def stacked_left(table):
    high, low = high_low(table)
    return np.concatenate(
        [
            np.concatenate([high, high], axis=-1),
            np.concatenate([low, np.zeros_like(low)], axis=-1),
        ],
        axis=-2,
    )


def root(product, modulus):
    angle = (product % modulus) * (-2.0 * np.pi / modulus)
    return np.cos(angle), np.sin(angle)


@functools.lru_cache(maxsize=None)
def tables():
    rows = np.arange(OUTER)
    limb = np.arange(OUTER)
    mid = np.arange(MID)
    lane = np.arange(LANES)
    kappa = np.concatenate([np.arange(0, MID, 2), np.arange(1, MID, 2)])
    bins = 2 * (lane % 64) + lane // 64
    first, first_back = [], []
    for place in range(ACC):
        own = rows[place * OWNED : place * OWNED + ROWS]
        real, imag = root(own[:, None] * limb[None, :], OUTER)
        empty = np.zeros((PADDED - 2 * ROWS, OUTER))
        first.append(stacked_left(np.concatenate([real, imag, empty], axis=0)))
        order = [(place + 2) % ACC, (place + 1) % ACC, (place + 3) % ACC, place]
        kept = np.concatenate([np.arange(8 * q, 8 * q + 8) for q in order])
        real, imag = root(kept[:, None] * own[None, :], OUTER)
        empty = np.zeros((len(kept), PADDED - 2 * ROWS))
        first_back.append(stacked_left(np.concatenate([real, imag, empty], axis=1) / LENGTH))
    freq = rows[:, None] + OUTER * kappa[None, :]
    real, imag = root(freq[:, :, None] * mid[None, None, :], 2048)
    second = stacked_left(
        np.concatenate(
            [np.concatenate([real, -imag], axis=2), np.concatenate([imag, real], axis=2)], axis=1
        )
    )
    real, imag = real.transpose(0, 2, 1), -imag.transpose(0, 2, 1)
    second_back = stacked_left(
        np.concatenate(
            [np.concatenate([real, -imag], axis=2), np.concatenate([imag, real], axis=2)], axis=1
        )
    )
    real, imag = root(freq[:, :, None] * lane[None, None, :], LENGTH)
    twiddle = np.stack([real, imag], axis=1).astype(np.float32)
    real, imag = root(lane[:, None] * bins[None, :], LANES)
    third = np.stack(
        high_low(
            np.concatenate(
                [np.concatenate([real, imag], axis=1), np.concatenate([-imag, real], axis=1)], axis=0
            )
        )
    )
    real, imag = real.T, -imag.T
    third_back = np.stack(
        high_low(
            np.concatenate(
                [np.concatenate([real, imag], axis=1), np.concatenate([-imag, real], axis=1)], axis=0
            )
        )
    )
    return (
        np.stack(first),
        second,
        twiddle,
        third,
        third_back,
        second_back,
        np.stack(first_back),
        np.concatenate([np.eye(LANES)[::-1]] * 2, axis=0).astype(ml_dtypes.bfloat16),
    )


def split(value):
    high = value.astype(jnp.bfloat16)
    low = (value - high.astype(jnp.float32)).astype(jnp.bfloat16)
    return high, low


def dot(first, second):
    return jnp.dot(first, second, preferred_element_type=jnp.float32)


def left_product(stacked, value):
    high, low = split(value)
    both = dot(stacked, jnp.concatenate([high, low], axis=0))
    rows = both.shape[0] // 2
    return both[:rows] + both[rows:]


def right_product(value, table):
    high, low = split(value)
    rows = value.shape[0]
    both = dot(jnp.concatenate([high, low], axis=0), table[0])
    return both[:rows] + both[rows:] + dot(high, table[1])


def exchanged(value, lower):
    top, bottom = value[: MID // 2], value[MID // 2 :]
    return jnp.concatenate(
        [
            jnp.where(lower, top, pltpu.roll(bottom, 64, 1)),
            jnp.where(lower, pltpu.roll(top, 64, 1), bottom),
        ],
        axis=0,
    )


def kernel(
    blocks,
    recip_hbm,
    limbs_hbm,
    first_hbm,
    second_hbm,
    twiddle_hbm,
    third_ref,
    third_back_ref,
    flip_ref,
    second_back_hbm,
    first_back_hbm,
    out_ref,
    recip,
    paired,
    flipped,
    weights,
    limbs,
    first,
    second,
    twiddle,
    second_back,
    first_back,
    mixed,
    spectra,
    crossing,
    back,
    result,
    transit,
    arrived,
    local_sem,
    over_send,
    over_recv,
    gather_send,
    gather_recv,
    share_send,
    share_recv,
    ring_send,
    ring_recv,
    leave_send,
    enter_send,
    cross_recv,
    sum_send,
    sum_recv,
):
    blk = lax.axis_index("blk")
    acc = lax.axis_index("acc")
    tail = lax.axis_index("tail")
    right = {"blk": blk, "acc": lax.rem(acc + 1, ACC), "tail": tail}
    left = {"blk": blk, "acc": lax.rem(acc + ACC - 1, ACC), "tail": tail}
    later = {"blk": lax.rem(blk + tail, blocks), "acc": acc, "tail": 1 - tail}
    earlier = {"blk": lax.rem(blk + blocks - 1 + tail, blocks), "acc": acc, "tail": 1 - tail}
    onward = {"blk": lax.rem(blk + 1, blocks), "acc": acc, "tail": tail}
    backward = {"blk": lax.rem(blk + blocks - 1, blocks), "acc": acc, "tail": tail}
    partner = {"blk": blk, "acc": ACC - 1 - acc, "tail": tail}
    cycle = min(CYCLE, blocks)
    spot = lax.rem(blk, cycle)
    core = lax.rem(blk, CORES)
    parity = lax.rem(spot // CORES, 2)
    mate = {"blk": blk + 1 - 2 * core, "acc": acc, "tail": tail}
    below = {"blk": blk - spot + lax.rem(spot + cycle - CORES, cycle), "acc": acc, "tail": tail}
    above = {"blk": blk - spot + lax.rem(spot + CORES, cycle), "acc": acc, "tail": tail}
    crosses = blocks > cycle
    makers = [spot == cycle - 1 - step for step in range(ROUNDS - 1)]
    vias = [spot == 1, None, spot == cycle // 2 - 1]
    to_via = [blocks - cycle + 2, None, cycle // 2 + 2]
    to_start = [cycle - 1, 2, blocks - cycle // 2 + 1]

    def along(steps):
        return {"blk": lax.rem(blk + steps, blocks), "acc": acc, "tail": tail}

    def remote(src, dst, send_sem, recv_sem, device):
        return pltpu.make_async_remote_copy(
            src_ref=src,
            dst_ref=dst,
            send_sem=send_sem,
            recv_sem=recv_sem,
            device_id=device,
            device_id_type=pl.DeviceIdType.MESH,
        )

    def quarter(part, owner, start, size):
        first_row = pl.multiple_of((part * ACC + owner) * QUARTER + start, HALF)
        return limbs.at[pl.ds(first_row, size)]

    barrier = pltpu.get_barrier_semaphore()
    for device in (right, left, later, earlier, onward, backward, below, above):
        pl.semaphore_signal(barrier, inc=1, device_id=device, device_id_type=pl.DeviceIdType.MESH)

    def greet(steps):
        pl.semaphore_signal(
            barrier,
            inc=1,
            device_id=along(blocks - steps),
            device_id_type=pl.DeviceIdType.MESH,
        )

    greeted = 8
    if crosses:
        for place in (*makers, vias[0], vias[2]):
            greeted += jnp.where(place, 1, 0)

        @pl.when(spot == 0)
        def _():
            for steps in to_start:
                greet(steps)

        for step in (0, 2):

            @pl.when(vias[step])
            def _():
                greet(to_via[step])

    own_rows = pl.ds(acc * OWNED, ROWS)
    own_limbs = pltpu.make_async_copy(limbs_hbm, quarter(0, acc, 0, QUARTER), local_sem.at[0])
    local = [
        pltpu.make_async_copy(first_hbm.at[acc], first, local_sem.at[1]),
        pltpu.make_async_copy(second_hbm.at[own_rows], second, local_sem.at[2]),
        pltpu.make_async_copy(twiddle_hbm.at[own_rows], twiddle, local_sem.at[3]),
        pltpu.make_async_copy(second_back_hbm.at[own_rows], second_back, local_sem.at[4]),
        pltpu.make_async_copy(first_back_hbm.at[acc], first_back, local_sem.at[5]),
        pltpu.make_async_copy(recip_hbm, recip, local_sem.at[6]),
    ]
    own_limbs.start()
    for copy in local:
        copy.start()
    own_limbs.wait()

    def clear(mid, carry):
        start = pl.multiple_of(mid * PADDED, PADDED)
        back[pl.ds(start + 16, PADDED - 16)] = jnp.zeros((PADDED - 16, LANES), jnp.float32)
        return carry

    lax.fori_loop(0, MID, clear, 0)
    pl.semaphore_wait(barrier, greeted)

    over = remote(
        quarter(0, acc, 0, QUARTER),
        quarter(1, acc, 0, QUARTER),
        over_send.at[0],
        over_recv.at[0],
        later,
    )
    over.start()

    def gather(part, step, owner, start, device):
        ref = quarter(part, owner, start, HALF)
        return remote(ref, ref, gather_send.at[part, step], gather_recv.at[part, step], device)

    from_left = lax.rem(acc + ACC - 1, ACC)
    from_right = lax.rem(acc + 1, ACC)

    def spread(part):
        steps = [
            gather(part, 0, acc, 0, right),
            gather(part, 1, acc, HALF, left),
            gather(part, 2, acc, HALF, right),
            gather(part, 3, acc, 0, left),
        ]
        for copy in steps:
            copy.start()
        return steps

    def pass_on(part, steps):
        steps[0].wait_recv()
        to_right = gather(part, 4, from_left, 0, right)
        to_right.start()
        steps[1].wait_recv()
        to_left = gather(part, 5, from_right, HALF, left)
        to_left.start()
        return [to_right, to_left]

    own_steps = spread(0)
    over.wait_recv()
    earlier_steps = spread(1)
    own_steps += pass_on(0, own_steps)
    earlier_steps += pass_on(1, earlier_steps)

    def share(step, source, round_index, device):
        found = []
        for side in range(2):
            start = pl.multiple_of(round_index * 1024 + side * 512 + 256, 256)
            slot = paired.at[round_index, side]
            found.append(
                remote(
                    recip_hbm.at[pl.ds(start, 256)] if source is None else slot,
                    slot,
                    share_send.at[step, side],
                    share_recv.at[step, side],
                    device,
                )
            )
        return found

    own_round = parity * 2 + core
    fetched = share(0, None, own_round, partner)
    to_mate = share(1, paired, own_round, mate)
    to_below = share(2, paired, own_round, below)
    relayed = share(3, paired, (1 - parity) * 2 + core, mate)
    for copy in fetched:
        copy.start()
    for copy in own_steps[2:] + earlier_steps[2:]:
        copy.wait_recv()
    for copy in local:
        copy.wait()

    lower = lax.broadcasted_iota(jnp.int32, (MID // 2, LANES), 1) < 64

    def first_step(turn, carry):
        values = [limbs[pl.ds(GROUP * turn + side, OUTER, stride=MID)] for side in range(GROUP)]
        product = left_product(first[...], jnp.concatenate(values, axis=1))
        for side in range(GROUP):
            start = pl.multiple_of((GROUP * turn + side) * PADDED, PADDED)
            mixed[pl.ds(start, PADDED)] = product[:, side * LANES : (side + 1) * LANES]
        return carry

    lax.fori_loop(0, MID // GROUP, first_step, 0)

    def chunk_of(step, chunk):
        return spectra.at[step, :, pl.ds(chunk * CHUNK, CHUNK)]

    def ring(step, chunk):
        return remote(
            chunk_of(step, chunk),
            chunk_of(step + 1, chunk),
            ring_send.at[step, chunk],
            ring_recv.at[step, chunk],
            onward,
        )

    def leave(step, chunk):
        if vias[step] is None:
            return remote(
                chunk_of(0, chunk),
                chunk_of(step + 1, chunk),
                leave_send.at[chunk],
                ring_recv.at[step, chunk],
                along(to_start[step]),
            )
        return remote(
            chunk_of(0, chunk),
            crossing.at[:, pl.ds(chunk * CHUNK, CHUNK)],
            leave_send.at[chunk],
            cross_recv.at[chunk],
            along(to_via[step]),
        )

    def enter(step, chunk):
        return remote(
            crossing.at[:, pl.ds(chunk * CHUNK, CHUNK)],
            chunk_of(step + 1, chunk),
            enter_send.at[chunk],
            ring_recv.at[step, chunk],
            along(to_start[step]),
        )

    def send_on(step, chunk):
        if crosses:

            @pl.when(jnp.logical_not(makers[0]))
            def _():
                ring(step, chunk).start()

        else:
            ring(step, chunk).start()

    def send_across(chunk):
        if crosses:
            for step in range(ROUNDS - 1):

                @pl.when(makers[step])
                def _():
                    leave(step, chunk).start()

    def help_across(chunk):
        if crosses:
            for step in (0, 2):

                @pl.when(vias[step])
                def _():
                    leave(step, chunk).wait_recv()
                    enter(step, chunk).start()

    def forward(chunk, carry):
        reals, imags = [], []
        for place in range(CHUNK):
            row = chunk * CHUNK + place
            value = jnp.concatenate(
                [
                    mixed[pl.ds(row, MID, stride=PADDED)],
                    mixed[pl.ds(ROWS + row, MID, stride=PADDED)],
                ],
                axis=0,
            )
            product = left_product(second[row], value)
            real, imag = product[:MID], product[MID:]
            turn_real, turn_imag = twiddle[row, 0], twiddle[row, 1]
            reals.append(real * turn_real - imag * turn_imag)
            imags.append(real * turn_imag + imag * turn_real)
        value = jnp.concatenate(
            [jnp.concatenate(reals, axis=0), jnp.concatenate(imags, axis=0)], axis=1
        )
        product = right_product(value, third_ref)
        for place in range(CHUNK):
            rows = product[place * MID : (place + 1) * MID]
            spectra[0, 0, chunk * CHUNK + place] = exchanged(rows[:, :LANES], lower)
            spectra[0, 1, chunk * CHUNK + place] = exchanged(rows[:, LANES:], lower)
        send_across(chunk)
        send_on(0, chunk)
        return carry

    lax.fori_loop(0, CHUNKS, forward, 0)

    for side in range(2):
        fetched[side].wait_recv()
        to_mate[side].start()
        to_below[side].start()

    def pass_ring(step):
        def body(chunk, carry):
            ring(step, chunk).wait_recv()
            send_on(step + 1, chunk)
            if step == 0:
                help_across(chunk)
            return carry

        lax.fori_loop(0, CHUNKS, body, 0)

    pass_ring(0)
    for side in range(2):
        to_below[side].wait_recv()
        relayed[side].start()
    pass_ring(1)
    for side in range(2):
        to_mate[side].wait_recv()
        relayed[side].wait_recv()

    def weigh(step, carry):
        for side in range(2):
            high, low = split(paired[step, side])
            turned = dot(jnp.concatenate([high, low], axis=1), flip_ref[...])
            for group in range(MID):
                flipped[side, pl.ds((MID - 1 - group) * 8, 8)] = turned[group * 8 : group * 8 + 8]
            start = step * 1024 + side * 512
            weights[step, side, 0] = recip[pl.ds(start, MID, stride=8)]
            weights[step, side, ROWS - 1] = recip[pl.ds(start + 256, MID, stride=8)]
            for row in range(1, ROWS - 1):
                own = recip[pl.ds(start + row, MID, stride=8)]
                other = flipped[side, pl.ds(8 - row, MID, stride=8)]
                weights[step, side, row] = own + other if side == 0 else own - other
        return carry

    lax.fori_loop(0, ROUNDS, weigh, 0)

    def arrive(chunk, carry):
        ring(2, chunk).wait_recv()
        reals, imags = [], []
        for place in range(CHUNK):
            row = chunk * CHUNK + place
            total_real = total_imag = None
            for step in range(ROUNDS):
                weight_real, weight_imag = weights[step, 0, row], weights[step, 1, row]
                real, imag = spectra[step, 0, row], spectra[step, 1, row]
                term_real = weight_real * real - weight_imag * imag
                term_imag = weight_real * imag + weight_imag * real
                total_real = term_real if step == 0 else total_real + term_real
                total_imag = term_imag if step == 0 else total_imag + term_imag
            reals.append(exchanged(total_real, lower))
            imags.append(exchanged(total_imag, lower))
        value = jnp.concatenate(
            [jnp.concatenate(reals, axis=0), jnp.concatenate(imags, axis=0)], axis=1
        )
        product = right_product(value, third_back_ref)
        for place in range(CHUNK):
            row = chunk * CHUNK + place
            real = product[place * MID : (place + 1) * MID, :LANES]
            imag = product[place * MID : (place + 1) * MID, LANES:]
            turn_real, turn_imag = twiddle[row, 0], twiddle[row, 1]
            turned = jnp.concatenate(
                [real * turn_real + imag * turn_imag, imag * turn_real - real * turn_imag], axis=0
            )
            unmixed = left_product(second_back[row], turned)
            back[pl.ds(row, MID, stride=PADDED)] = unmixed[:MID]
            back[pl.ds(ROWS + row, MID, stride=PADDED)] = unmixed[MID:]
        return carry

    lax.fori_loop(0, CHUNKS, arrive, 0)

    def last_step(turn, carry):
        values = []
        for side in range(GROUP):
            start = pl.multiple_of((GROUP * turn + side) * PADDED, PADDED)
            values.append(back[pl.ds(start, PADDED)])
        product = left_product(first_back[...], jnp.concatenate(values, axis=1))
        for side in range(GROUP):
            result[pl.ds(GROUP * turn + side, MID, stride=MID)] = product[
                :, side * LANES : (side + 1) * LANES
            ]
        return carry

    lax.fori_loop(0, MID // GROUP, last_step, 0)

    def part(place, start):
        return result.at[pl.ds(place * QUARTER + start, HALF)]

    to_right = remote(part(0, 0), transit.at[0], sum_send.at[0], sum_recv.at[0], right)
    to_left = remote(part(0, HALF), transit.at[1], sum_send.at[1], sum_recv.at[1], left)
    plain_right = remote(part(1, HALF), arrived.at[0], sum_send.at[2], sum_recv.at[2], right)
    plain_left = remote(part(2, 0), arrived.at[1], sum_send.at[3], sum_recv.at[3], left)
    summed_right = remote(part(1, 0), arrived.at[2], sum_send.at[4], sum_recv.at[4], right)
    summed_left = remote(part(2, HALF), arrived.at[3], sum_send.at[5], sum_recv.at[5], left)
    to_right.start()
    to_left.start()
    plain_right.start()
    plain_left.start()
    to_right.wait_recv()
    result[QUARTER : QUARTER + HALF] += transit[0]
    summed_right.start()
    to_left.wait_recv()
    result[2 * QUARTER + HALF : 3 * QUARTER] += transit[1]
    summed_left.start()
    plain_right.wait_recv()
    plain_left.wait_recv()
    summed_right.wait_recv()
    out_ref[:HALF] = result[3 * QUARTER : 3 * QUARTER + HALF] + arrived[1] + arrived[2]
    summed_left.wait_recv()
    out_ref[HALF:] = result[3 * QUARTER + HALF :] + arrived[0] + arrived[3]

    sent = [over, *own_steps, *earlier_steps]
    sent += [*fetched, *to_mate, *to_below, *relayed]
    sent += [to_right, to_left, plain_right, plain_left, summed_right, summed_left]
    for copy in sent:
        copy.wait_send()

    def drain(chunk, carry):
        if crosses:
            for step in range(ROUNDS - 1):

                @pl.when(makers[step])
                def _():
                    leave(step, chunk).wait_send()

            for step in (0, 2):

                @pl.when(vias[step])
                def _():
                    enter(step, chunk).wait_send()

            @pl.when(jnp.logical_not(makers[0]))
            def _():
                for step in range(ROUNDS - 1):
                    ring(step, chunk).wait_send()

        else:
            for step in range(ROUNDS - 1):
                ring(step, chunk).wait_send()

        return carry

    lax.fori_loop(0, CHUNKS, drain, 0)


def per_device(blocks, reciprocal_spectra, divisor):
    recip = reciprocal_spectra.reshape(ROUNDS, 2, 2, 8, MID, LANES)
    recip = recip.transpose(0, 1, 2, 4, 3, 5).reshape(ROUNDS * 1024, LANES)
    limbs = divisor.reshape(QUARTER, LANES)
    constants = [jnp.asarray(table) for table in tables()]
    first, second, twiddle, third, third_back, second_back, first_back, flip = constants
    anywhere = pl.BlockSpec(memory_space=pl.ANY)
    vmem = pl.BlockSpec(memory_space=pltpu.VMEM)
    out = pl.pallas_call(
        functools.partial(kernel, blocks),
        out_shape=jax.ShapeDtypeStruct((QUARTER, LANES), jnp.float32),
        in_specs=[anywhere] * 5 + [vmem] * 3 + [anywhere] * 2,
        out_specs=vmem,
        scratch_shapes=[
            pltpu.VMEM((ROUNDS * 1024, LANES), jnp.float32),
            pltpu.VMEM((ROUNDS, 2, QUARTER, LANES), jnp.float32),
            pltpu.VMEM((2, QUARTER, LANES), jnp.float32),
            pltpu.VMEM((ROUNDS, 2, ROWS, MID, LANES), jnp.float32),
            pltpu.VMEM((2 * ACC * QUARTER, LANES), jnp.float32),
            pltpu.VMEM(first.shape[1:], jnp.bfloat16),
            pltpu.VMEM((ROWS, *second.shape[1:]), jnp.bfloat16),
            pltpu.VMEM((ROWS, *twiddle.shape[1:]), jnp.float32),
            pltpu.VMEM((ROWS, *second_back.shape[1:]), jnp.bfloat16),
            pltpu.VMEM(first_back.shape[1:], jnp.bfloat16),
            pltpu.VMEM((MID * PADDED, LANES), jnp.float32),
            pltpu.VMEM((ROUNDS, 2, ROWS, MID, LANES), jnp.float32),
            pltpu.VMEM((2, ROWS, MID, LANES), jnp.float32),
            pltpu.VMEM((MID * PADDED, LANES), jnp.float32),
            pltpu.VMEM((ACC * QUARTER, LANES), jnp.float32),
            pltpu.VMEM((2, HALF, LANES), jnp.float32),
            pltpu.VMEM((4, HALF, LANES), jnp.float32),
            pltpu.SemaphoreType.DMA((7,)),
            pltpu.SemaphoreType.DMA((1,)),
            pltpu.SemaphoreType.DMA((1,)),
            pltpu.SemaphoreType.DMA((2, 6)),
            pltpu.SemaphoreType.DMA((2, 6)),
            pltpu.SemaphoreType.DMA((4, 2)),
            pltpu.SemaphoreType.DMA((4, 2)),
            pltpu.SemaphoreType.DMA((ROUNDS - 1, CHUNKS)),
            pltpu.SemaphoreType.DMA((ROUNDS - 1, CHUNKS)),
            pltpu.SemaphoreType.DMA((CHUNKS,)),
            pltpu.SemaphoreType.DMA((CHUNKS,)),
            pltpu.SemaphoreType.DMA((CHUNKS,)),
            pltpu.SemaphoreType.DMA((6,)),
            pltpu.SemaphoreType.DMA((6,)),
        ],
        compiler_params=pltpu.CompilerParams(
            collective_id=0, has_side_effects=True, vmem_limit_bytes=60 * 1024 * 1024
        ),
    )(recip, limbs, first, second, twiddle, third, third_back, flip, second_back, first_back)
    return out.reshape(1, QUARTER * LANES)


def solution(mesh):
    in_specs = (P(None, None, "acc", None), P(("blk", "tail"), "acc"))
    out_specs = P(("blk", "tail"), "acc")
    return jax.shard_map(
        functools.partial(per_device, mesh.shape["blk"]),
        mesh=mesh,
        in_specs=in_specs,
        out_specs=out_specs,
        check_vma=False,
    )
```

```python
import functools

import jax
import jax.numpy as jnp
import ml_dtypes
import numpy as np
from jax import lax
from jax.experimental import pallas as pl
from jax.experimental.pallas import tpu as pltpu
from jax.sharding import PartitionSpec as P

LENGTH = 262144
ACC = 4
OWNED = 16
ROWS = 9
LIMB_ROWS = 32
PIECES = 2
PIECE = 256 // PIECES
PADDED = 32
OUTER = 64
MID = 32
LANES = 128
QUARTER = 256
HALF = QUARTER // 2
CHUNK = 3
CHUNKS = ROWS // CHUNK
ROUNDS = 4
CORES = 2
GROUP = 8
CYCLE = 16


def high_low(table):
    high = table.astype(ml_dtypes.bfloat16)
    low = (table - high.astype(np.float64)).astype(ml_dtypes.bfloat16)
    return high, low


def stacked_left(table):
    high, low = high_low(table)
    return np.concatenate(
        [
            np.concatenate([high, high], axis=-1),
            np.concatenate([low, np.zeros_like(low)], axis=-1),
        ],
        axis=-2,
    )


def root(product, modulus):
    angle = (product % modulus) * (-2.0 * np.pi / modulus)
    return np.cos(angle), np.sin(angle)


def rows_of(place):
    odd = place // 2
    own = OWNED * place + 2 * np.arange(8) + odd
    return np.append(own, own[0] if odd else OWNED * (ACC - 1 - place))


@functools.lru_cache(maxsize=None)
def tables():
    rows = np.stack([rows_of(place) for place in range(ACC)])
    limb = np.arange(LIMB_ROWS)
    mid = np.arange(MID)
    lane = np.arange(LANES)
    kappa = np.concatenate([np.arange(0, MID, 2), np.arange(1, MID, 2)])
    bins = 2 * (lane % 64) + lane // 64
    first, first_back = [], []
    for place in range(ACC):
        own = rows[place]
        real, imag = root(own[:, None] * limb[None, :], OUTER)
        empty = np.zeros((PADDED - 2 * ROWS, LIMB_ROWS))
        first.append(stacked_left(np.concatenate([real, imag, empty], axis=0)))
        order = [(place + 2) % ACC, (place + 1) % ACC, (place + 3) % ACC, place]
        kept = np.concatenate([np.arange(8 * q, 8 * q + 8) for q in order])
        real, imag = root(kept[:, None] * own[None, :], OUTER)
        empty = np.zeros((len(kept), PADDED - 2 * ROWS))
        first_back.append(stacked_left(np.concatenate([real, imag, empty], axis=1) / LENGTH))
    freq = rows[:, :, None] + OUTER * kappa
    real, imag = root(freq[..., None] * mid, 2048)
    second = stacked_left(
        np.concatenate(
            [np.concatenate([real, -imag], axis=-1), np.concatenate([imag, real], axis=-1)], axis=-2
        )
    )
    real, imag = real.swapaxes(-1, -2), -imag.swapaxes(-1, -2)
    second_back = stacked_left(
        np.concatenate(
            [np.concatenate([real, -imag], axis=-1), np.concatenate([imag, real], axis=-1)], axis=-2
        )
    )
    real, imag = root(freq[..., None] * lane, LENGTH)
    twiddle = np.stack([real, imag], axis=2).astype(np.float32)
    real, imag = root(lane[:, None] * bins[None, :], LANES)
    third = np.stack(
        high_low(
            np.concatenate(
                [np.concatenate([real, imag], axis=1), np.concatenate([-imag, real], axis=1)], axis=0
            )
        )
    )
    real, imag = real.T, -imag.T
    third_back = np.stack(
        high_low(
            np.concatenate(
                [np.concatenate([real, imag], axis=1), np.concatenate([-imag, real], axis=1)], axis=0
            )
        )
    )
    return (
        np.stack(first),
        second,
        twiddle,
        third,
        third_back,
        second_back,
        np.stack(first_back),
        np.concatenate([np.eye(LANES)[::-1]] * 2, axis=0).astype(ml_dtypes.bfloat16),
    )


def split(value):
    high = value.astype(jnp.bfloat16)
    low = (value - high.astype(jnp.float32)).astype(jnp.bfloat16)
    return high, low


def dot(first, second):
    return jnp.dot(first, second, preferred_element_type=jnp.float32)


def left_product(stacked, value):
    high, low = split(value)
    both = dot(stacked, jnp.concatenate([high, low], axis=0))
    rows = both.shape[0] // 2
    return both[:rows] + both[rows:]


def right_product(value, table):
    high, low = split(value)
    rows = value.shape[0]
    both = dot(jnp.concatenate([high, low], axis=0), table[0])
    return both[:rows] + both[rows:] + dot(high, table[1])


def exchanged(value, lower):
    top, bottom = value[: MID // 2], value[MID // 2 :]
    return jnp.concatenate(
        [
            jnp.where(lower, top, pltpu.roll(bottom, 64, 1)),
            jnp.where(lower, pltpu.roll(top, 64, 1), bottom),
        ],
        axis=0,
    )


def kernel(
    blocks,
    recip_hbm,
    limbs_hbm,
    first_hbm,
    second_hbm,
    twiddle_hbm,
    third_hbm,
    third_back_hbm,
    flip_hbm,
    second_back_hbm,
    first_back_hbm,
    out_ref,
    recip,
    paired,
    packed,
    flipped,
    weights,
    own,
    prior,
    other,
    limbs,
    first,
    second,
    twiddle,
    third,
    third_back,
    flip,
    second_back,
    first_back,
    mixed,
    spectra,
    crossing,
    back,
    result,
    transit,
    arrived,
    local_sem,
    over_send,
    over_recv,
    gather_send,
    gather_recv,
    share_send,
    share_recv,
    ring_send,
    ring_recv,
    leave_send,
    enter_send,
    cross_recv,
    sum_send,
    sum_recv,
    ready,
):
    blk = lax.axis_index("blk")
    acc = lax.axis_index("acc")
    tail = lax.axis_index("tail")
    right = {"blk": blk, "acc": lax.rem(acc + 1, ACC), "tail": tail}
    left = {"blk": blk, "acc": lax.rem(acc + ACC - 1, ACC), "tail": tail}
    later = {"blk": lax.rem(blk + tail, blocks), "acc": acc, "tail": 1 - tail}
    earlier = {"blk": lax.rem(blk + blocks - 1 + tail, blocks), "acc": acc, "tail": 1 - tail}
    onward = {"blk": lax.rem(blk + 1, blocks), "acc": acc, "tail": tail}
    backward = {"blk": lax.rem(blk + blocks - 1, blocks), "acc": acc, "tail": tail}
    odd = acc // 2
    pair = ACC - 1 - acc
    twin = acc + 1 - 2 * lax.rem(acc, 2)
    beside = {"blk": blk, "acc": twin, "tail": tail}
    partner = {"blk": blk, "acc": ACC - 1 - acc, "tail": tail}
    cycle = min(CYCLE, blocks)
    spot = lax.rem(blk, cycle)
    core = lax.rem(blk, CORES)
    parity = lax.rem(spot // CORES, 2)
    across = {"blk": blk, "acc": acc, "tail": 1 - tail}
    mate = {"blk": blk + 1 - 2 * core, "acc": acc, "tail": tail}
    below = {"blk": blk - spot + lax.rem(spot + cycle - CORES, cycle), "acc": acc, "tail": tail}
    above = {"blk": blk - spot + lax.rem(spot + CORES, cycle), "acc": acc, "tail": tail}
    crosses = blocks > cycle
    makers = [spot == cycle - 1 - step for step in range(ROUNDS - 1)]
    vias = [spot == 1, None, spot == cycle // 2 - 1]
    to_via = [blocks - cycle + 2, None, cycle // 2 + 2]
    to_start = [cycle - 1, 2, blocks - cycle // 2 + 1]

    def along(steps):
        return {"blk": lax.rem(blk + steps, blocks), "acc": acc, "tail": tail}

    def remote(src, dst, send_sem, recv_sem, device):
        return pltpu.make_async_remote_copy(
            src_ref=src,
            dst_ref=dst,
            send_sem=send_sem,
            recv_sem=recv_sem,
            device_id=device,
            device_id_type=pl.DeviceIdType.MESH,
        )

    def quarter(owner, piece):
        return limbs.at[pl.ds(pl.multiple_of(owner * QUARTER + piece * PIECE, PIECE), PIECE)]

    barrier = pltpu.get_barrier_semaphore()
    for device in (right, left, earlier, backward, mate, across, below):
        pl.semaphore_signal(barrier, inc=1, device_id=device, device_id_type=pl.DeviceIdType.MESH)

    def greet(steps):
        pl.semaphore_signal(
            barrier,
            inc=1,
            device_id=along(blocks - steps),
            device_id_type=pl.DeviceIdType.MESH,
        )

    greeted = 7
    if crosses:
        for place in (*makers, vias[0], vias[2]):
            greeted += jnp.where(place, 1, 0)

        @pl.when(spot == 0)
        def _():
            for steps in to_start:
                greet(steps)

        for step in (0, 2):

            @pl.when(vias[step])
            def _():
                greet(to_via[step])

    own_limbs = pltpu.make_async_copy(limbs_hbm, own, local_sem.at[0])
    local = [
        pltpu.make_async_copy(first_hbm.at[acc], first, local_sem.at[1]),
        pltpu.make_async_copy(second_hbm.at[acc], second, local_sem.at[2]),
        pltpu.make_async_copy(twiddle_hbm.at[acc], twiddle, local_sem.at[3]),
        pltpu.make_async_copy(second_back_hbm.at[acc], second_back, local_sem.at[4]),
        pltpu.make_async_copy(first_back_hbm.at[acc], first_back, local_sem.at[5]),
        pltpu.make_async_copy(third_hbm, third, local_sem.at[7]),
        pltpu.make_async_copy(third_back_hbm, third_back, local_sem.at[8]),
        pltpu.make_async_copy(flip_hbm, flip, local_sem.at[9]),
    ]
    own_recip = pltpu.make_async_copy(recip_hbm, recip, local_sem.at[6])
    own_limbs.start()
    own_recip.start()
    for copy in local:
        copy.start()
    own_limbs.wait()

    def clear(mid, carry):
        start = pl.multiple_of(mid * PADDED, PADDED)
        back[pl.ds(start + 16, PADDED - 16)] = jnp.zeros((PADDED - 16, LANES), jnp.float32)
        return carry

    lax.fori_loop(0, MID, clear, 0)
    pl.semaphore_wait(barrier, greeted)
    pl.semaphore_signal(ready, inc=1, device_id=above, device_id_type=pl.DeviceIdType.MESH)

    over = [
        remote(
            own.at[pl.ds(piece * PIECE, PIECE)],
            prior.at[pl.ds(piece * PIECE, PIECE)],
            over_send.at[piece],
            over_recv.at[piece],
            later,
        )
        for piece in range(PIECES)
    ]
    for copy in over:
        copy.start()

    def gather(step, piece, source, owner, device):
        return remote(
            source,
            quarter(owner, piece),
            gather_send.at[step, piece],
            gather_recv.at[step, piece],
            device,
        )

    pieces = range(PIECES)
    to_pair = [
        gather(0, piece, other.at[pl.ds(piece * PIECE, PIECE)], acc, partner) for piece in pieces
    ]
    to_twin = [gather(1, piece, quarter(acc, piece), acc, beside) for piece in pieces]
    passed = [gather(2, piece, quarter(pair, piece), pair, beside) for piece in pieces]

    def start_row(odd_row, row):
        return (row // 4) * 256 + 2 * (row % 4) + odd_row

    own_round = parity * 2 + tail
    own_recip.wait()
    for row in range(8):
        start = own_round * 1024 + core * 512 + start_row(1 - odd, row)
        packed[pl.ds(row, MID, stride=8)] = recip[pl.ds(start, MID, stride=8)]

    def share(step, round_index, device):
        slot = paired.at[round_index, core]
        return remote(
            packed if step == 0 else slot,
            slot,
            share_send.at[step],
            share_recv.at[step],
            device,
        )

    across_round = parity * 2 + 1 - tail
    above_round = (1 - parity) * 2 + tail
    far_round = (1 - parity) * 2 + 1 - tail
    fetched = share(0, own_round, partner)
    own_to_mate = share(1, own_round, mate)
    own_across = share(2, own_round, across)
    own_below = share(3, own_round, below)
    across_to_mate = share(4, across_round, mate)
    across_below = share(5, across_round, below)
    above_to_mate = share(6, above_round, mate)
    far_to_mate = share(7, far_round, mate)
    fetched.start()
    sign = (1 - 2 * odd).astype(jnp.float32)
    for piece in pieces:
        rows = pl.ds(piece * PIECE, PIECE)
        over[piece].wait_recv()
        signed = prior[rows] * sign
        other[rows] = own[rows] - signed
        to_pair[piece].start()
        limbs[pl.ds(pl.multiple_of(acc * QUARTER + piece * PIECE, PIECE), PIECE)] = (
            own[rows] + signed
        )
        to_twin[piece].start()
    for piece in pieces:
        to_pair[piece].wait_recv()
        passed[piece].start()
    fetched.wait_recv()
    own_across.start()
    pl.semaphore_wait(ready, 1)
    own_below.start()
    own_to_mate.start()
    for copy in to_twin + passed:
        copy.wait_recv()
    for copy in local:
        copy.wait()

    lower = lax.broadcasted_iota(jnp.int32, (MID // 2, LANES), 1) < 64

    def first_step(turn, carry):
        values = [limbs[pl.ds(GROUP * turn + side, LIMB_ROWS, stride=MID)] for side in range(GROUP)]
        product = left_product(first[...], jnp.concatenate(values, axis=1))
        for side in range(GROUP):
            start = pl.multiple_of((GROUP * turn + side) * PADDED, PADDED)
            mixed[pl.ds(start, PADDED)] = product[:, side * LANES : (side + 1) * LANES]
        return carry

    lax.fori_loop(0, MID // GROUP, first_step, 0)
    own_across.wait_recv()
    across_below.start()
    across_to_mate.start()
    own_below.wait_recv()
    above_to_mate.start()

    def chunk_of(step, chunk):
        return spectra.at[step, :, pl.ds(chunk * CHUNK, CHUNK)]

    def ring(step, chunk):
        return remote(
            chunk_of(step, chunk),
            chunk_of(step + 1, chunk),
            ring_send.at[step, chunk],
            ring_recv.at[step, chunk],
            onward,
        )

    def leave(step, chunk):
        if vias[step] is None:
            return remote(
                chunk_of(0, chunk),
                chunk_of(step + 1, chunk),
                leave_send.at[chunk],
                ring_recv.at[step, chunk],
                along(to_start[step]),
            )
        return remote(
            chunk_of(0, chunk),
            crossing.at[:, pl.ds(chunk * CHUNK, CHUNK)],
            leave_send.at[chunk],
            cross_recv.at[chunk],
            along(to_via[step]),
        )

    def enter(step, chunk):
        return remote(
            crossing.at[:, pl.ds(chunk * CHUNK, CHUNK)],
            chunk_of(step + 1, chunk),
            enter_send.at[chunk],
            ring_recv.at[step, chunk],
            along(to_start[step]),
        )

    def send_on(step, chunk):
        if crosses:

            @pl.when(jnp.logical_not(makers[0]))
            def _():
                ring(step, chunk).start()

        else:
            ring(step, chunk).start()

    def send_across(chunk):
        if crosses:
            for step in range(ROUNDS - 1):

                @pl.when(makers[step])
                def _():
                    leave(step, chunk).start()

    def help_across(chunk):
        if crosses:
            for step in (0, 2):

                @pl.when(vias[step])
                def _():
                    leave(step, chunk).wait_recv()
                    enter(step, chunk).start()

    def forward(chunk, carry):
        reals, imags = [], []
        for place in range(CHUNK):
            row = chunk * CHUNK + place
            value = jnp.concatenate(
                [
                    mixed[pl.ds(row, MID, stride=PADDED)],
                    mixed[pl.ds(ROWS + row, MID, stride=PADDED)],
                ],
                axis=0,
            )
            product = left_product(second[row], value)
            real, imag = product[:MID], product[MID:]
            turn_real, turn_imag = twiddle[row, 0], twiddle[row, 1]
            reals.append(real * turn_real - imag * turn_imag)
            imags.append(real * turn_imag + imag * turn_real)
        value = jnp.concatenate(
            [jnp.concatenate(reals, axis=0), jnp.concatenate(imags, axis=0)], axis=1
        )
        product = right_product(value, third)
        for place in range(CHUNK):
            rows = product[place * MID : (place + 1) * MID]
            spectra[0, 0, chunk * CHUNK + place] = exchanged(rows[:, :LANES], lower)
            spectra[0, 1, chunk * CHUNK + place] = exchanged(rows[:, LANES:], lower)
        send_across(chunk)
        send_on(0, chunk)
        return carry

    lax.fori_loop(0, CHUNKS, forward, 0)
    across_below.wait_recv()
    far_to_mate.start()
    for copy in (own_to_mate, across_to_mate, above_to_mate, far_to_mate):
        copy.wait_recv()

    def pass_ring(step):
        def body(chunk, carry):
            ring(step, chunk).wait_recv()
            send_on(step + 1, chunk)
            if step == 0:
                help_across(chunk)
            return carry

        lax.fori_loop(0, CHUNKS, body, 0)

    def weigh(step, carry):
        for side in range(2):
            high, low = split(paired[step, side])
            turned = dot(jnp.concatenate([high, low], axis=1), flip[...])
            for group in range(MID):
                flipped[side, pl.ds((MID - 1 - group) * 8, 8)] = turned[group * 8 : group * 8 + 8]
            start = step * 1024 + side * 512
            for row in range(ROWS - 1):
                mine = recip[pl.ds(start + start_row(odd, row), MID, stride=8)]
                mirrored = 7 if row == 0 else 8 - row - odd
                theirs = flipped[side, pl.ds(mirrored, MID, stride=8)]
                if row == 0:
                    theirs = jnp.where(odd == 1, theirs, 0.0)
                weights[step, side, row] = mine + theirs if side == 0 else mine - theirs
            extra = paired[step, side, pl.ds(0, MID, stride=8)]
            weights[step, side, ROWS - 1] = jnp.where(odd == 1, 0.0, extra)
        return carry

    lax.fori_loop(0, ROUNDS, weigh, 0)
    pass_ring(0)
    pass_ring(1)

    def arrive(chunk, carry):
        ring(2, chunk).wait_recv()
        reals, imags = [], []
        for place in range(CHUNK):
            row = chunk * CHUNK + place
            total_real = total_imag = None
            for step in range(ROUNDS):
                weight_real, weight_imag = weights[step, 0, row], weights[step, 1, row]
                real, imag = spectra[step, 0, row], spectra[step, 1, row]
                term_real = weight_real * real - weight_imag * imag
                term_imag = weight_real * imag + weight_imag * real
                total_real = term_real if step == 0 else total_real + term_real
                total_imag = term_imag if step == 0 else total_imag + term_imag
            reals.append(exchanged(total_real, lower))
            imags.append(exchanged(total_imag, lower))
        value = jnp.concatenate(
            [jnp.concatenate(reals, axis=0), jnp.concatenate(imags, axis=0)], axis=1
        )
        product = right_product(value, third_back)
        for place in range(CHUNK):
            row = chunk * CHUNK + place
            real = product[place * MID : (place + 1) * MID, :LANES]
            imag = product[place * MID : (place + 1) * MID, LANES:]
            turn_real, turn_imag = twiddle[row, 0], twiddle[row, 1]
            turned = jnp.concatenate(
                [real * turn_real + imag * turn_imag, imag * turn_real - real * turn_imag], axis=0
            )
            unmixed = left_product(second_back[row], turned)
            back[pl.ds(row, MID, stride=PADDED)] = unmixed[:MID]
            back[pl.ds(ROWS + row, MID, stride=PADDED)] = unmixed[MID:]
        return carry

    lax.fori_loop(0, CHUNKS, arrive, 0)

    def last_step(turn, carry):
        values = []
        for side in range(GROUP):
            start = pl.multiple_of((GROUP * turn + side) * PADDED, PADDED)
            values.append(back[pl.ds(start, PADDED)])
        product = left_product(first_back[...], jnp.concatenate(values, axis=1))
        for side in range(GROUP):
            result[pl.ds(GROUP * turn + side, MID, stride=MID)] = product[
                :, side * LANES : (side + 1) * LANES
            ]
        return carry

    lax.fori_loop(0, MID // GROUP, last_step, 0)

    def part(place, start):
        return result.at[pl.ds(place * QUARTER + start, HALF)]

    to_right = remote(part(0, 0), transit.at[0], sum_send.at[0], sum_recv.at[0], right)
    to_left = remote(part(0, HALF), transit.at[1], sum_send.at[1], sum_recv.at[1], left)
    plain_right = remote(part(1, HALF), arrived.at[0], sum_send.at[2], sum_recv.at[2], right)
    plain_left = remote(part(2, 0), arrived.at[1], sum_send.at[3], sum_recv.at[3], left)
    summed_right = remote(part(1, 0), arrived.at[2], sum_send.at[4], sum_recv.at[4], right)
    summed_left = remote(part(2, HALF), arrived.at[3], sum_send.at[5], sum_recv.at[5], left)
    to_right.start()
    to_left.start()
    to_right.wait_send()
    plain_right.start()
    to_left.wait_send()
    plain_left.start()
    to_right.wait_recv()
    result[QUARTER : QUARTER + HALF] += transit[0]
    summed_right.start()
    to_left.wait_recv()
    result[2 * QUARTER + HALF : 3 * QUARTER] += transit[1]
    summed_left.start()
    plain_right.wait_recv()
    plain_left.wait_recv()
    summed_right.wait_recv()
    out_ref[:HALF] = result[3 * QUARTER : 3 * QUARTER + HALF] + arrived[1] + arrived[2]
    summed_left.wait_recv()
    out_ref[HALF:] = result[3 * QUARTER + HALF :] + arrived[0] + arrived[3]

    sent = [*over, *to_pair, *to_twin, *passed]
    sent += [fetched, own_to_mate, own_across, own_below, across_to_mate, across_below]
    sent += [above_to_mate, far_to_mate]
    sent += [plain_right, plain_left, summed_right, summed_left]
    for copy in sent:
        copy.wait_send()

    def drain(chunk, carry):
        if crosses:
            for step in range(ROUNDS - 1):

                @pl.when(makers[step])
                def _():
                    leave(step, chunk).wait_send()

            for step in (0, 2):

                @pl.when(vias[step])
                def _():
                    enter(step, chunk).wait_send()

            @pl.when(jnp.logical_not(makers[0]))
            def _():
                for step in range(ROUNDS - 1):
                    ring(step, chunk).wait_send()

        else:
            for step in range(ROUNDS - 1):
                ring(step, chunk).wait_send()

        return carry

    lax.fori_loop(0, CHUNKS, drain, 0)


def per_device(blocks, reciprocal_spectra, divisor):
    recip = reciprocal_spectra.reshape(ROUNDS, 2, 2, 8, MID, LANES)
    recip = recip.transpose(0, 1, 2, 4, 3, 5).reshape(ROUNDS * 1024, LANES)
    limbs = divisor.reshape(QUARTER, LANES)
    constants = [jnp.asarray(table) for table in tables()]
    first, second, twiddle, third, third_back, second_back, first_back, flip = constants
    anywhere = pl.BlockSpec(memory_space=pl.ANY)
    vmem = pl.BlockSpec(memory_space=pltpu.VMEM)
    out = pl.pallas_call(
        functools.partial(kernel, blocks),
        out_shape=jax.ShapeDtypeStruct((QUARTER, LANES), jnp.float32),
        in_specs=[anywhere] * 10,
        out_specs=vmem,
        scratch_shapes=[
            pltpu.VMEM((ROUNDS * 1024, LANES), jnp.float32),
            pltpu.VMEM((ROUNDS, 2, QUARTER, LANES), jnp.float32),
            pltpu.VMEM((QUARTER, LANES), jnp.float32),
            pltpu.VMEM((2, QUARTER, LANES), jnp.float32),
            pltpu.VMEM((ROUNDS, 2, ROWS, MID, LANES), jnp.float32),
            *[pltpu.VMEM((QUARTER, LANES), jnp.float32)] * 3,
            pltpu.VMEM((ACC * QUARTER, LANES), jnp.float32),
            pltpu.VMEM(first.shape[1:], jnp.bfloat16),
            pltpu.VMEM(second.shape[1:], jnp.bfloat16),
            pltpu.VMEM(twiddle.shape[1:], jnp.float32),
            pltpu.VMEM(third.shape, jnp.bfloat16),
            pltpu.VMEM(third_back.shape, jnp.bfloat16),
            pltpu.VMEM(flip.shape, jnp.bfloat16),
            pltpu.VMEM(second_back.shape[1:], jnp.bfloat16),
            pltpu.VMEM(first_back.shape[1:], jnp.bfloat16),
            pltpu.VMEM((MID * PADDED, LANES), jnp.float32),
            pltpu.VMEM((ROUNDS, 2, ROWS, MID, LANES), jnp.float32),
            pltpu.VMEM((2, ROWS, MID, LANES), jnp.float32),
            pltpu.VMEM((MID * PADDED, LANES), jnp.float32),
            pltpu.VMEM((ACC * QUARTER, LANES), jnp.float32),
            pltpu.VMEM((2, HALF, LANES), jnp.float32),
            pltpu.VMEM((4, HALF, LANES), jnp.float32),
            pltpu.SemaphoreType.DMA((10,)),
            pltpu.SemaphoreType.DMA((PIECES,)),
            pltpu.SemaphoreType.DMA((PIECES,)),
            pltpu.SemaphoreType.DMA((3, PIECES)),
            pltpu.SemaphoreType.DMA((3, PIECES)),
            pltpu.SemaphoreType.DMA((8,)),
            pltpu.SemaphoreType.DMA((8,)),
            pltpu.SemaphoreType.DMA((ROUNDS - 1, CHUNKS)),
            pltpu.SemaphoreType.DMA((ROUNDS - 1, CHUNKS)),
            pltpu.SemaphoreType.DMA((CHUNKS,)),
            pltpu.SemaphoreType.DMA((CHUNKS,)),
            pltpu.SemaphoreType.DMA((CHUNKS,)),
            pltpu.SemaphoreType.DMA((6,)),
            pltpu.SemaphoreType.DMA((6,)),
            pltpu.SemaphoreType.REGULAR,
        ],
        compiler_params=pltpu.CompilerParams(
            collective_id=0, has_side_effects=True, vmem_limit_bytes=60 * 1024 * 1024
        ),
    )(recip, limbs, first, second, twiddle, third, third_back, flip, second_back, first_back)
    return out.reshape(1, QUARTER * LANES)


def solution(mesh):
    in_specs = (P(None, None, "acc", None), P(("blk", "tail"), "acc"))
    out_specs = P(("blk", "tail"), "acc")
    return jax.shard_map(
        functools.partial(per_device, mesh.shape["blk"]),
        mesh=mesh,
        in_specs=in_specs,
        out_specs=out_specs,
        check_vma=False,
    )
```

```python
import functools

import jax
import jax.numpy as jnp
import ml_dtypes
import numpy as np
from jax import lax
from jax.experimental import pallas as pl
from jax.experimental.pallas import tpu as pltpu
from jax.sharding import PartitionSpec as P

LENGTH = 262144
ACC = 4
OWNED = 16
ROWS = 9
LIMB_ROWS = 32
PIECES = 2
PIECE = 256 // PIECES
PADDED = 32
OUTER = 64
MID = 32
LANES = 128
QUARTER = 256
HALF = QUARTER // 2
CHUNK = 3
CHUNKS = ROWS // CHUNK
ROUNDS = 4
CORES = 2
GROUP = 16
CYCLE = 16


def high_low(table):
    high = table.astype(ml_dtypes.bfloat16)
    low = (table - high.astype(np.float64)).astype(ml_dtypes.bfloat16)
    return high, low


def stacked_left(table):
    high, low = high_low(table)
    return np.concatenate(
        [
            np.concatenate([high, high], axis=-1),
            np.concatenate([low, np.zeros_like(low)], axis=-1),
        ],
        axis=-2,
    )


def root(product, modulus):
    angle = (product % modulus) * (-2.0 * np.pi / modulus)
    return np.cos(angle), np.sin(angle)


def rows_of(place):
    odd = place // 2
    own = OWNED * place + 2 * np.arange(8) + odd
    return np.append(own, own[0] if odd else OWNED * (ACC - 1 - place))


@functools.lru_cache(maxsize=None)
def tables():
    rows = np.stack([rows_of(place) for place in range(ACC)])
    limb = np.arange(LIMB_ROWS)
    mid = np.arange(MID)
    lane = np.arange(LANES)
    kappa = np.concatenate([np.arange(0, MID, 2), np.arange(1, MID, 2)])
    bins = 2 * (lane % 64) + lane // 64
    first, first_back = [], []
    for place in range(ACC):
        own = rows[place]
        real, imag = root(own[:, None] * limb[None, :], OUTER)
        empty = np.zeros((PADDED - 2 * ROWS, LIMB_ROWS))
        first.append(stacked_left(np.concatenate([real, imag, empty], axis=0)))
        order = [(place + 2) % ACC, (place + 1) % ACC, (place + 3) % ACC, place]
        kept = np.concatenate([np.arange(8 * q, 8 * q + 8) for q in order])
        real, imag = root(kept[:, None] * own[None, :], OUTER)
        empty = np.zeros((len(kept), PADDED - 2 * ROWS))
        first_back.append(stacked_left(np.concatenate([real, imag, empty], axis=1) / LENGTH))
    freq = rows[:, :, None] + OUTER * kappa
    real, imag = root(freq[..., None] * mid, 2048)
    second = stacked_left(
        np.concatenate(
            [np.concatenate([real, -imag], axis=-1), np.concatenate([imag, real], axis=-1)], axis=-2
        )
    )
    real, imag = real.swapaxes(-1, -2), -imag.swapaxes(-1, -2)
    second_back = stacked_left(
        np.concatenate(
            [np.concatenate([real, -imag], axis=-1), np.concatenate([imag, real], axis=-1)], axis=-2
        )
    )
    real, imag = root(freq[..., None] * lane, LENGTH)
    twiddle = np.stack([real, imag], axis=2).astype(np.float32)
    real, imag = root(lane[:, None] * bins[None, :], LANES)
    third = np.stack(
        high_low(
            np.concatenate(
                [np.concatenate([real, imag], axis=1), np.concatenate([-imag, real], axis=1)], axis=0
            )
        )
    )
    real, imag = real.T, -imag.T
    third_back = np.stack(
        high_low(
            np.concatenate(
                [np.concatenate([real, imag], axis=1), np.concatenate([-imag, real], axis=1)], axis=0
            )
        )
    )
    return (
        np.stack(first),
        second,
        twiddle,
        third,
        third_back,
        second_back,
        np.stack(first_back),
        np.concatenate([np.eye(LANES)[::-1]] * 2, axis=0).astype(ml_dtypes.bfloat16),
    )


def split(value):
    high = value.astype(jnp.bfloat16)
    low = (value - high.astype(jnp.float32)).astype(jnp.bfloat16)
    return high, low


def dot(first, second):
    return jnp.dot(first, second, preferred_element_type=jnp.float32)


def left_product(stacked, value):
    high, low = split(value)
    both = dot(stacked, jnp.concatenate([high, low], axis=0))
    rows = both.shape[0] // 2
    return both[:rows] + both[rows:]


def right_product(value, table):
    high, low = split(value)
    rows = value.shape[0]
    both = dot(jnp.concatenate([high, low], axis=0), table[0])
    return both[:rows] + both[rows:] + dot(high, table[1])


def exchanged(value, lower):
    top, bottom = value[: MID // 2], value[MID // 2 :]
    return jnp.concatenate(
        [
            jnp.where(lower, top, pltpu.roll(bottom, 64, 1)),
            jnp.where(lower, pltpu.roll(top, 64, 1), bottom),
        ],
        axis=0,
    )


def kernel(
    blocks,
    recip_hbm,
    limbs_hbm,
    first_hbm,
    second_hbm,
    twiddle_hbm,
    third_hbm,
    third_back_hbm,
    flip_hbm,
    second_back_hbm,
    first_back_hbm,
    out_ref,
    more_ref,
    recip,
    paired,
    packed,
    flipped,
    weights,
    own,
    prior,
    other,
    limbs,
    first,
    second,
    twiddle,
    third,
    third_back,
    flip,
    second_back,
    first_back,
    mixed,
    spectra,
    crossing,
    back,
    result,
    transit,
    arrived,
    local_sem,
    over_send,
    over_recv,
    gather_send,
    gather_recv,
    share_send,
    share_recv,
    ring_send,
    ring_recv,
    leave_send,
    enter_send,
    cross_recv,
    sum_send,
    sum_recv,
    ready,
):
    blk = lax.axis_index("blk")
    acc = lax.axis_index("acc")
    tail = lax.axis_index("tail")
    right = {"blk": blk, "acc": lax.rem(acc + 1, ACC), "tail": tail}
    left = {"blk": blk, "acc": lax.rem(acc + ACC - 1, ACC), "tail": tail}
    later = {"blk": lax.rem(blk + tail, blocks), "acc": acc, "tail": 1 - tail}
    earlier = {"blk": lax.rem(blk + blocks - 1 + tail, blocks), "acc": acc, "tail": 1 - tail}
    onward = {"blk": lax.rem(blk + 1, blocks), "acc": acc, "tail": tail}
    backward = {"blk": lax.rem(blk + blocks - 1, blocks), "acc": acc, "tail": tail}
    odd = acc // 2
    pair = ACC - 1 - acc
    twin = acc + 1 - 2 * lax.rem(acc, 2)
    beside = {"blk": blk, "acc": twin, "tail": tail}
    partner = {"blk": blk, "acc": ACC - 1 - acc, "tail": tail}
    cycle = min(CYCLE, blocks)
    spot = lax.rem(blk, cycle)
    core = lax.rem(blk, CORES)
    parity = lax.rem(spot // CORES, 2)
    across = {"blk": blk, "acc": acc, "tail": 1 - tail}
    mate = {"blk": blk + 1 - 2 * core, "acc": acc, "tail": tail}
    below = {"blk": blk - spot + lax.rem(spot + cycle - CORES, cycle), "acc": acc, "tail": tail}
    above = {"blk": blk - spot + lax.rem(spot + CORES, cycle), "acc": acc, "tail": tail}
    crosses = blocks > cycle
    makers = [spot == cycle - 1 - step for step in range(ROUNDS - 1)]
    vias = [spot == 1, None, spot == cycle // 2 - 1]
    to_via = [blocks - cycle + 2, None, cycle // 2 + 2]
    to_start = [cycle - 1, 2, blocks - cycle // 2 + 1]

    def along(steps):
        return {"blk": lax.rem(blk + steps, blocks), "acc": acc, "tail": tail}

    def remote(src, dst, send_sem, recv_sem, device):
        return pltpu.make_async_remote_copy(
            src_ref=src,
            dst_ref=dst,
            send_sem=send_sem,
            recv_sem=recv_sem,
            device_id=device,
            device_id_type=pl.DeviceIdType.MESH,
        )

    def quarter(owner, piece):
        return limbs.at[pl.ds(pl.multiple_of(owner * QUARTER + piece * PIECE, PIECE), PIECE)]

    barrier = pltpu.get_barrier_semaphore()
    for device in (right, left, earlier, backward, mate, across, below):
        pl.semaphore_signal(barrier, inc=1, device_id=device, device_id_type=pl.DeviceIdType.MESH)

    def greet(steps):
        pl.semaphore_signal(
            barrier,
            inc=1,
            device_id=along(blocks - steps),
            device_id_type=pl.DeviceIdType.MESH,
        )

    greeted = 7
    if crosses:
        for place in (*makers, vias[0], vias[2]):
            greeted += jnp.where(place, 1, 0)

        @pl.when(spot == 0)
        def _():
            for steps in to_start:
                greet(steps)

        for step in (0, 2):

            @pl.when(vias[step])
            def _():
                greet(to_via[step])

    own_limbs = pltpu.make_async_copy(limbs_hbm, own, local_sem.at[0])
    local = [
        pltpu.make_async_copy(first_hbm.at[acc], first, local_sem.at[1]),
        pltpu.make_async_copy(second_hbm.at[acc], second, local_sem.at[2]),
        pltpu.make_async_copy(twiddle_hbm.at[acc], twiddle, local_sem.at[3]),
        pltpu.make_async_copy(second_back_hbm.at[acc], second_back, local_sem.at[4]),
        pltpu.make_async_copy(first_back_hbm.at[acc], first_back, local_sem.at[5]),
        pltpu.make_async_copy(third_hbm, third, local_sem.at[7]),
        pltpu.make_async_copy(third_back_hbm, third_back, local_sem.at[8]),
        pltpu.make_async_copy(flip_hbm, flip, local_sem.at[9]),
    ]
    own_recip = pltpu.make_async_copy(recip_hbm, recip, local_sem.at[6])
    own_limbs.start()
    own_recip.start()
    for copy in local:
        copy.start()
    own_limbs.wait()

    def clear(mid, carry):
        start = pl.multiple_of(mid * PADDED, PADDED)
        back[pl.ds(start + 16, PADDED - 16)] = jnp.zeros((PADDED - 16, LANES), jnp.float32)
        return carry

    lax.fori_loop(0, MID, clear, 0)
    pl.semaphore_wait(barrier, greeted)
    pl.semaphore_signal(ready, inc=1, device_id=above, device_id_type=pl.DeviceIdType.MESH)

    over = [
        remote(
            own.at[pl.ds(piece * PIECE, PIECE)],
            prior.at[pl.ds(piece * PIECE, PIECE)],
            over_send.at[piece],
            over_recv.at[piece],
            later,
        )
        for piece in range(PIECES)
    ]
    for copy in over:
        copy.start()

    def gather(step, piece, source, owner, device):
        return remote(
            source,
            quarter(owner, piece),
            gather_send.at[step, piece],
            gather_recv.at[step, piece],
            device,
        )

    pieces = range(PIECES)
    to_pair = [
        gather(0, piece, other.at[pl.ds(piece * PIECE, PIECE)], acc, partner) for piece in pieces
    ]
    to_twin = [gather(1, piece, quarter(acc, piece), acc, beside) for piece in pieces]
    passed = [gather(2, piece, quarter(pair, piece), pair, beside) for piece in pieces]

    def start_row(odd_row, row):
        return (row // 4) * 256 + 2 * (row % 4) + odd_row

    own_round = parity * 2 + tail
    own_recip.wait()
    for row in range(8):
        start = own_round * 1024 + core * 512 + start_row(1 - odd, row)
        packed[pl.ds(row, MID, stride=8)] = recip[pl.ds(start, MID, stride=8)]

    def share(step, round_index, device):
        slot = paired.at[round_index, core]
        return remote(
            packed if step == 0 else slot,
            slot,
            share_send.at[step],
            share_recv.at[step],
            device,
        )

    across_round = parity * 2 + 1 - tail
    above_round = (1 - parity) * 2 + tail
    far_round = (1 - parity) * 2 + 1 - tail
    fetched = share(0, own_round, partner)
    own_to_mate = share(1, own_round, mate)
    own_across = share(2, own_round, across)
    own_below = share(3, own_round, below)
    across_to_mate = share(4, across_round, mate)
    across_below = share(5, across_round, below)
    above_to_mate = share(6, above_round, mate)
    far_to_mate = share(7, far_round, mate)
    fetched.start()

    def pass_fetched():
        fetched.wait_recv()
        own_across.start()
        own_to_mate.start()

    late = jnp.logical_and(spot == 0, tail == 0)
    pl.when(late)(pass_fetched)
    sign = (1 - 2 * odd).astype(jnp.float32)
    for piece in pieces:
        rows = pl.ds(piece * PIECE, PIECE)
        over[piece].wait_recv()
        signed = prior[rows] * sign
        other[rows] = own[rows] - signed
        to_pair[piece].start()
        limbs[pl.ds(pl.multiple_of(acc * QUARTER + piece * PIECE, PIECE), PIECE)] = (
            own[rows] + signed
        )
        to_twin[piece].start()
    for piece in pieces:
        to_pair[piece].wait_recv()
        passed[piece].start()
    pl.when(jnp.logical_not(late))(pass_fetched)
    pl.semaphore_wait(ready, 1)
    own_below.start()
    for copy in to_twin + passed:
        copy.wait_recv()
    for copy in local:
        copy.wait()

    lower = lax.broadcasted_iota(jnp.int32, (MID // 2, LANES), 1) < 64

    def first_step(turn, carry):
        values = [limbs[pl.ds(GROUP * turn + side, LIMB_ROWS, stride=MID)] for side in range(GROUP)]
        product = left_product(first[...], jnp.concatenate(values, axis=1))
        for side in range(GROUP):
            start = pl.multiple_of((GROUP * turn + side) * PADDED, PADDED)
            mixed[pl.ds(start, PADDED)] = product[:, side * LANES : (side + 1) * LANES]
        return carry

    lax.fori_loop(0, MID // GROUP, first_step, 0)
    own_across.wait_recv()
    across_below.start()
    across_to_mate.start()
    own_below.wait_recv()
    above_to_mate.start()

    def chunk_of(step, chunk):
        return spectra.at[step, :, pl.ds(chunk * CHUNK, CHUNK)]

    def ring(step, chunk):
        return remote(
            chunk_of(step, chunk),
            chunk_of(step + 1, chunk),
            ring_send.at[step, chunk],
            ring_recv.at[step, chunk],
            onward,
        )

    def leave(step, chunk):
        if vias[step] is None:
            return remote(
                chunk_of(0, chunk),
                chunk_of(step + 1, chunk),
                leave_send.at[chunk],
                ring_recv.at[step, chunk],
                along(to_start[step]),
            )
        return remote(
            chunk_of(0, chunk),
            crossing.at[:, pl.ds(chunk * CHUNK, CHUNK)],
            leave_send.at[chunk],
            cross_recv.at[chunk],
            along(to_via[step]),
        )

    def enter(step, chunk):
        return remote(
            crossing.at[:, pl.ds(chunk * CHUNK, CHUNK)],
            chunk_of(step + 1, chunk),
            enter_send.at[chunk],
            ring_recv.at[step, chunk],
            along(to_start[step]),
        )

    def send_on(step, chunk):
        if crosses:

            @pl.when(jnp.logical_not(makers[0]))
            def _():
                ring(step, chunk).start()

        else:
            ring(step, chunk).start()

    def send_across(chunk):
        if crosses:
            for step in range(ROUNDS - 1):

                @pl.when(makers[step])
                def _():
                    leave(step, chunk).start()

    def help_across(chunk):
        if crosses:
            for step in (0, 2):

                @pl.when(vias[step])
                def _():
                    leave(step, chunk).wait_recv()
                    enter(step, chunk).start()

    def forward(chunk, carry):
        reals, imags = [], []
        for place in range(CHUNK):
            row = chunk * CHUNK + place
            value = jnp.concatenate(
                [
                    mixed[pl.ds(row, MID, stride=PADDED)],
                    mixed[pl.ds(ROWS + row, MID, stride=PADDED)],
                ],
                axis=0,
            )
            product = left_product(second[row], value)
            real, imag = product[:MID], product[MID:]
            turn_real, turn_imag = twiddle[row, 0], twiddle[row, 1]
            reals.append(real * turn_real - imag * turn_imag)
            imags.append(real * turn_imag + imag * turn_real)
        value = jnp.concatenate(
            [jnp.concatenate(reals, axis=0), jnp.concatenate(imags, axis=0)], axis=1
        )
        product = right_product(value, third)
        for place in range(CHUNK):
            rows = product[place * MID : (place + 1) * MID]
            spectra[0, 0, chunk * CHUNK + place] = exchanged(rows[:, :LANES], lower)
            spectra[0, 1, chunk * CHUNK + place] = exchanged(rows[:, LANES:], lower)
        send_across(chunk)
        send_on(0, chunk)
        return carry

    lax.fori_loop(0, CHUNKS, forward, 0)
    across_below.wait_recv()
    far_to_mate.start()
    for copy in (own_to_mate, across_to_mate, above_to_mate, far_to_mate):
        copy.wait_recv()

    def pass_ring(step):
        def body(chunk, carry):
            ring(step, chunk).wait_recv()
            send_on(step + 1, chunk)
            if step == 0:
                help_across(chunk)
            return carry

        lax.fori_loop(0, CHUNKS, body, 0)

    def weigh(step, carry):
        for side in range(2):
            high, low = split(paired[step, side])
            turned = dot(jnp.concatenate([high, low], axis=1), flip[...])
            for group in range(MID):
                flipped[side, pl.ds((MID - 1 - group) * 8, 8)] = turned[group * 8 : group * 8 + 8]
            start = step * 1024 + side * 512
            for row in range(ROWS - 1):
                mine = recip[pl.ds(start + start_row(odd, row), MID, stride=8)]
                mirrored = 7 if row == 0 else 8 - row - odd
                theirs = flipped[side, pl.ds(mirrored, MID, stride=8)]
                if row == 0:
                    theirs = jnp.where(odd == 1, theirs, 0.0)
                weights[step, side, row] = mine + theirs if side == 0 else mine - theirs
            extra = paired[step, side, pl.ds(0, MID, stride=8)]
            weights[step, side, ROWS - 1] = jnp.where(odd == 1, 0.0, extra)
        return carry

    lax.fori_loop(0, ROUNDS, weigh, 0)
    pass_ring(0)
    pass_ring(1)

    def arrive(chunk, carry):
        ring(2, chunk).wait_recv()
        reals, imags = [], []
        for place in range(CHUNK):
            row = chunk * CHUNK + place
            total_real = total_imag = None
            for step in range(ROUNDS):
                weight_real, weight_imag = weights[step, 0, row], weights[step, 1, row]
                real, imag = spectra[step, 0, row], spectra[step, 1, row]
                term_real = weight_real * real - weight_imag * imag
                term_imag = weight_real * imag + weight_imag * real
                total_real = term_real if step == 0 else total_real + term_real
                total_imag = term_imag if step == 0 else total_imag + term_imag
            reals.append(exchanged(total_real, lower))
            imags.append(exchanged(total_imag, lower))
        value = jnp.concatenate(
            [jnp.concatenate(reals, axis=0), jnp.concatenate(imags, axis=0)], axis=1
        )
        product = right_product(value, third_back)
        for place in range(CHUNK):
            row = chunk * CHUNK + place
            real = product[place * MID : (place + 1) * MID, :LANES]
            imag = product[place * MID : (place + 1) * MID, LANES:]
            turn_real, turn_imag = twiddle[row, 0], twiddle[row, 1]
            turned = jnp.concatenate(
                [real * turn_real + imag * turn_imag, imag * turn_real - real * turn_imag], axis=0
            )
            unmixed = left_product(second_back[row], turned)
            back[pl.ds(row, MID, stride=PADDED)] = unmixed[:MID]
            back[pl.ds(ROWS + row, MID, stride=PADDED)] = unmixed[MID:]
        return carry

    lax.fori_loop(0, CHUNKS, arrive, 0)

    def last_step(turn, carry):
        values = []
        for side in range(GROUP):
            start = pl.multiple_of((GROUP * turn + side) * PADDED, PADDED)
            values.append(back[pl.ds(start, PADDED)])
        product = left_product(first_back[...], jnp.concatenate(values, axis=1))
        for side in range(GROUP):
            result[pl.ds(GROUP * turn + side, MID, stride=MID)] = product[
                :, side * LANES : (side + 1) * LANES
            ]
        return carry

    lax.fori_loop(0, MID // GROUP, last_step, 0)

    def part(place, start):
        return result.at[pl.ds(place * QUARTER + start, HALF)]

    to_right = remote(part(0, 0), transit.at[0], sum_send.at[0], sum_recv.at[0], right)
    to_left = remote(part(0, HALF), transit.at[1], sum_send.at[1], sum_recv.at[1], left)
    plain_right = remote(part(1, HALF), arrived.at[0], sum_send.at[2], sum_recv.at[2], right)
    plain_left = remote(part(2, 0), arrived.at[1], sum_send.at[3], sum_recv.at[3], left)
    summed_right = remote(part(1, 0), arrived.at[2], sum_send.at[4], sum_recv.at[4], right)
    summed_left = remote(part(2, HALF), arrived.at[3], sum_send.at[5], sum_recv.at[5], left)
    to_right.start()
    to_left.start()
    plain_right.start()
    plain_left.start()
    to_right.wait_recv()
    result[QUARTER : QUARTER + HALF] += transit[0]
    summed_right.start()
    to_left.wait_recv()
    result[2 * QUARTER + HALF : 3 * QUARTER] += transit[1]
    summed_left.start()
    out_ref[...] = result[3 * QUARTER :]
    plain_right.wait_recv()
    out_ref[HALF:] += arrived[0]
    plain_left.wait_recv()
    out_ref[:HALF] += arrived[1]
    summed_right.wait_recv()
    more_ref[:HALF] = arrived[2]
    summed_left.wait_recv()
    more_ref[HALF:] = arrived[3]

    sent = [*over, *to_pair, *to_twin, *passed]
    sent += [fetched, own_to_mate, own_across, own_below, across_to_mate, across_below]
    sent += [above_to_mate, far_to_mate]
    sent += [to_right, to_left, plain_right, plain_left, summed_right, summed_left]
    for copy in sent:
        copy.wait_send()

    def drain(chunk, carry):
        if crosses:
            for step in range(ROUNDS - 1):

                @pl.when(makers[step])
                def _():
                    leave(step, chunk).wait_send()

            for step in (0, 2):

                @pl.when(vias[step])
                def _():
                    enter(step, chunk).wait_send()

            @pl.when(jnp.logical_not(makers[0]))
            def _():
                for step in range(ROUNDS - 1):
                    ring(step, chunk).wait_send()

        else:
            for step in range(ROUNDS - 1):
                ring(step, chunk).wait_send()

        return carry

    lax.fori_loop(0, CHUNKS, drain, 0)


def per_device(blocks, reciprocal_spectra, divisor):
    recip = reciprocal_spectra.reshape(ROUNDS, 2, 2, 8, MID, LANES)
    recip = recip.transpose(0, 1, 2, 4, 3, 5).reshape(ROUNDS * 1024, LANES)
    limbs = divisor.reshape(QUARTER, LANES)
    constants = [jnp.asarray(table) for table in tables()]
    first, second, twiddle, third, third_back, second_back, first_back, flip = constants
    anywhere = pl.BlockSpec(memory_space=pl.ANY)
    vmem = pl.BlockSpec(memory_space=pltpu.VMEM)
    kept, added = pl.pallas_call(
        functools.partial(kernel, blocks),
        out_shape=[jax.ShapeDtypeStruct((QUARTER, LANES), jnp.float32)] * 2,
        in_specs=[anywhere] * 10,
        out_specs=[vmem, vmem],
        scratch_shapes=[
            pltpu.VMEM((ROUNDS * 1024, LANES), jnp.float32),
            pltpu.VMEM((ROUNDS, 2, QUARTER, LANES), jnp.float32),
            pltpu.VMEM((QUARTER, LANES), jnp.float32),
            pltpu.VMEM((2, QUARTER, LANES), jnp.float32),
            pltpu.VMEM((ROUNDS, 2, ROWS, MID, LANES), jnp.float32),
            *[pltpu.VMEM((QUARTER, LANES), jnp.float32)] * 3,
            pltpu.VMEM((ACC * QUARTER, LANES), jnp.float32),
            pltpu.VMEM(first.shape[1:], jnp.bfloat16),
            pltpu.VMEM(second.shape[1:], jnp.bfloat16),
            pltpu.VMEM(twiddle.shape[1:], jnp.float32),
            pltpu.VMEM(third.shape, jnp.bfloat16),
            pltpu.VMEM(third_back.shape, jnp.bfloat16),
            pltpu.VMEM(flip.shape, jnp.bfloat16),
            pltpu.VMEM(second_back.shape[1:], jnp.bfloat16),
            pltpu.VMEM(first_back.shape[1:], jnp.bfloat16),
            pltpu.VMEM((MID * PADDED, LANES), jnp.float32),
            pltpu.VMEM((ROUNDS, 2, ROWS, MID, LANES), jnp.float32),
            pltpu.VMEM((2, ROWS, MID, LANES), jnp.float32),
            pltpu.VMEM((MID * PADDED, LANES), jnp.float32),
            pltpu.VMEM((ACC * QUARTER, LANES), jnp.float32),
            pltpu.VMEM((2, HALF, LANES), jnp.float32),
            pltpu.VMEM((4, HALF, LANES), jnp.float32),
            pltpu.SemaphoreType.DMA((10,)),
            pltpu.SemaphoreType.DMA((PIECES,)),
            pltpu.SemaphoreType.DMA((PIECES,)),
            pltpu.SemaphoreType.DMA((3, PIECES)),
            pltpu.SemaphoreType.DMA((3, PIECES)),
            pltpu.SemaphoreType.DMA((8,)),
            pltpu.SemaphoreType.DMA((8,)),
            pltpu.SemaphoreType.DMA((ROUNDS - 1, CHUNKS)),
            pltpu.SemaphoreType.DMA((ROUNDS - 1, CHUNKS)),
            pltpu.SemaphoreType.DMA((CHUNKS,)),
            pltpu.SemaphoreType.DMA((CHUNKS,)),
            pltpu.SemaphoreType.DMA((CHUNKS,)),
            pltpu.SemaphoreType.DMA((6,)),
            pltpu.SemaphoreType.DMA((6,)),
            pltpu.SemaphoreType.REGULAR,
        ],
        compiler_params=pltpu.CompilerParams(
            collective_id=0, has_side_effects=True, vmem_limit_bytes=60 * 1024 * 1024
        ),
    )(recip, limbs, first, second, twiddle, third, third_back, flip, second_back, first_back)
    return kept.reshape(1, QUARTER * LANES) + added.reshape(1, QUARTER * LANES)


def solution(mesh):
    in_specs = (P(None, None, "acc", None), P(("blk", "tail"), "acc"))
    out_specs = P(("blk", "tail"), "acc")
    return jax.shard_map(
        functools.partial(per_device, mesh.shape["blk"]),
        mesh=mesh,
        in_specs=in_specs,
        out_specs=out_specs,
        check_vma=False,
    )
```

```python
import functools

import jax
import jax.numpy as jnp
import ml_dtypes
import numpy as np
from jax import lax
from jax.experimental import pallas as pl
from jax.experimental.pallas import tpu as pltpu
from jax.sharding import PartitionSpec as P

LENGTH = 262144
ACC = 4
OWNED = 16
ROWS = 9
LIMB_ROWS = 32
PIECES = 2
PIECE = 256 // PIECES
PADDED = 32
OUTER = 64
MID = 32
LANES = 128
QUARTER = 256
HALF = QUARTER // 2
CHUNK = 3
CHUNKS = ROWS // CHUNK
ROUNDS = 4
CORES = 2
GROUP = 16
CYCLE = 16


def high_low(table):
    high = table.astype(ml_dtypes.bfloat16)
    low = (table - high.astype(np.float64)).astype(ml_dtypes.bfloat16)
    return high, low


def stacked_left(table):
    high, low = high_low(table)
    return np.concatenate(
        [
            np.concatenate([high, high], axis=-1),
            np.concatenate([low, np.zeros_like(low)], axis=-1),
        ],
        axis=-2,
    )


def root(product, modulus):
    angle = (product % modulus) * (-2.0 * np.pi / modulus)
    return np.cos(angle), np.sin(angle)


def rows_of(place):
    odd = place // 2
    own = OWNED * place + 2 * np.arange(8) + odd
    return np.append(own, own[0] if odd else OWNED * (ACC - 1 - place))


@functools.lru_cache(maxsize=None)
def tables():
    rows = np.stack([rows_of(place) for place in range(ACC)])
    limb = np.arange(LIMB_ROWS)
    mid = np.arange(MID)
    lane = np.arange(LANES)
    kappa = np.concatenate([np.arange(0, MID, 2), np.arange(1, MID, 2)])
    bins = 2 * (lane % 64) + lane // 64
    first, first_back = [], []
    for place in range(ACC):
        own = rows[place]
        real, imag = root(own[:, None] * limb[None, :], OUTER)
        empty = np.zeros((PADDED - 2 * ROWS, LIMB_ROWS))
        first.append(stacked_left(np.concatenate([real, imag, empty], axis=0)))
        order = [(place + 2) % ACC, (place + 1) % ACC, (place + 3) % ACC, place]
        kept = np.concatenate([np.arange(8 * q, 8 * q + 8) for q in order])
        real, imag = root(kept[:, None] * own[None, :], OUTER)
        empty = np.zeros((len(kept), PADDED - 2 * ROWS))
        table = np.concatenate([real, imag, empty], axis=1) / LENGTH
        first_back.append(
            np.concatenate([stacked_left(table[:8]), stacked_left(table[8:])], axis=0)
        )
    freq = rows[:, :, None] + OUTER * kappa
    real, imag = root(freq[..., None] * mid, 2048)
    second = stacked_left(
        np.concatenate(
            [np.concatenate([real, -imag], axis=-1), np.concatenate([imag, real], axis=-1)], axis=-2
        )
    )
    real, imag = real.swapaxes(-1, -2), -imag.swapaxes(-1, -2)
    second_back = stacked_left(
        np.concatenate(
            [np.concatenate([real, -imag], axis=-1), np.concatenate([imag, real], axis=-1)], axis=-2
        )
    )
    real, imag = root(freq[..., None] * lane, LENGTH)
    twiddle = np.stack([real, imag], axis=2).astype(np.float32)
    real, imag = root(lane[:, None] * bins[None, :], LANES)
    third = np.stack(
        high_low(
            np.concatenate(
                [np.concatenate([real, imag], axis=1), np.concatenate([-imag, real], axis=1)], axis=0
            )
        )
    )
    real, imag = real.T, -imag.T
    third_back = np.stack(
        high_low(
            np.concatenate(
                [np.concatenate([real, imag], axis=1), np.concatenate([-imag, real], axis=1)], axis=0
            )
        )
    )
    return (
        np.stack(first),
        second,
        twiddle,
        third,
        third_back,
        second_back,
        np.stack(first_back),
        np.concatenate([np.eye(LANES)[::-1]] * 2, axis=0).astype(ml_dtypes.bfloat16),
    )


def split(value):
    high = value.astype(jnp.bfloat16)
    low = (value - high.astype(jnp.float32)).astype(jnp.bfloat16)
    return high, low


def dot(first, second):
    return jnp.dot(first, second, preferred_element_type=jnp.float32)


def left_product(stacked, value):
    high, low = split(value)
    both = dot(stacked, jnp.concatenate([high, low], axis=0))
    rows = both.shape[0] // 2
    return both[:rows] + both[rows:]


def right_product(value, table):
    high, low = split(value)
    rows = value.shape[0]
    both = dot(jnp.concatenate([high, low], axis=0), table[0])
    return both[:rows] + both[rows:] + dot(high, table[1])


def exchanged(value, lower):
    top, bottom = value[: MID // 2], value[MID // 2 :]
    return jnp.concatenate(
        [
            jnp.where(lower, top, pltpu.roll(bottom, 64, 1)),
            jnp.where(lower, pltpu.roll(top, 64, 1), bottom),
        ],
        axis=0,
    )


def kernel(
    blocks,
    recip_hbm,
    limbs_hbm,
    first_hbm,
    second_hbm,
    twiddle_hbm,
    third_hbm,
    third_back_hbm,
    flip_hbm,
    second_back_hbm,
    first_back_hbm,
    out_ref,
    more_ref,
    recip,
    paired,
    packed,
    flipped,
    weights,
    own,
    prior,
    other,
    limbs,
    first,
    second,
    twiddle,
    third,
    third_back,
    flip,
    second_back,
    first_back,
    mixed,
    spectra,
    crossing,
    back,
    result,
    opposed,
    transit,
    arrived,
    local_sem,
    over_send,
    over_recv,
    gather_send,
    gather_recv,
    share_send,
    share_recv,
    ring_send,
    ring_recv,
    leave_send,
    enter_send,
    cross_recv,
    sum_send,
    sum_recv,
    ready,
):
    blk = lax.axis_index("blk")
    acc = lax.axis_index("acc")
    tail = lax.axis_index("tail")
    right = {"blk": blk, "acc": lax.rem(acc + 1, ACC), "tail": tail}
    left = {"blk": blk, "acc": lax.rem(acc + ACC - 1, ACC), "tail": tail}
    later = {"blk": lax.rem(blk + tail, blocks), "acc": acc, "tail": 1 - tail}
    earlier = {"blk": lax.rem(blk + blocks - 1 + tail, blocks), "acc": acc, "tail": 1 - tail}
    onward = {"blk": lax.rem(blk + 1, blocks), "acc": acc, "tail": tail}
    backward = {"blk": lax.rem(blk + blocks - 1, blocks), "acc": acc, "tail": tail}
    odd = acc // 2
    pair = ACC - 1 - acc
    twin = acc + 1 - 2 * lax.rem(acc, 2)
    beside = {"blk": blk, "acc": twin, "tail": tail}
    partner = {"blk": blk, "acc": ACC - 1 - acc, "tail": tail}
    cycle = min(CYCLE, blocks)
    spot = lax.rem(blk, cycle)
    core = lax.rem(blk, CORES)
    parity = lax.rem(spot // CORES, 2)
    across = {"blk": blk, "acc": acc, "tail": 1 - tail}
    mate = {"blk": blk + 1 - 2 * core, "acc": acc, "tail": tail}
    below = {"blk": blk - spot + lax.rem(spot + cycle - CORES, cycle), "acc": acc, "tail": tail}
    above = {"blk": blk - spot + lax.rem(spot + CORES, cycle), "acc": acc, "tail": tail}
    crosses = blocks > cycle
    makers = [spot == cycle - 1 - step for step in range(ROUNDS - 1)]
    vias = [spot == 1, None, spot == cycle // 2 - 1]
    to_via = [blocks - cycle + 2, None, cycle // 2 + 2]
    to_start = [cycle - 1, 2, blocks - cycle // 2 + 1]

    def along(steps):
        return {"blk": lax.rem(blk + steps, blocks), "acc": acc, "tail": tail}

    def remote(src, dst, send_sem, recv_sem, device):
        return pltpu.make_async_remote_copy(
            src_ref=src,
            dst_ref=dst,
            send_sem=send_sem,
            recv_sem=recv_sem,
            device_id=device,
            device_id_type=pl.DeviceIdType.MESH,
        )

    def quarter(owner, piece):
        return limbs.at[pl.ds(pl.multiple_of(owner * QUARTER + piece * PIECE, PIECE), PIECE)]

    barrier = pltpu.get_barrier_semaphore()
    for device in (right, left, earlier, backward, mate, across, below):
        pl.semaphore_signal(barrier, inc=1, device_id=device, device_id_type=pl.DeviceIdType.MESH)

    def greet(steps):
        pl.semaphore_signal(
            barrier,
            inc=1,
            device_id=along(blocks - steps),
            device_id_type=pl.DeviceIdType.MESH,
        )

    greeted = 7
    if crosses:
        for place in (*makers, vias[0], vias[2]):
            greeted += jnp.where(place, 1, 0)

        @pl.when(spot == 0)
        def _():
            for steps in to_start:
                greet(steps)

        for step in (0, 2):

            @pl.when(vias[step])
            def _():
                greet(to_via[step])

    own_limbs = pltpu.make_async_copy(limbs_hbm, own, local_sem.at[0])
    local = [
        pltpu.make_async_copy(first_hbm.at[acc], first, local_sem.at[1]),
        pltpu.make_async_copy(second_hbm.at[acc], second, local_sem.at[2]),
        pltpu.make_async_copy(twiddle_hbm.at[acc], twiddle, local_sem.at[3]),
        pltpu.make_async_copy(second_back_hbm.at[acc], second_back, local_sem.at[4]),
        pltpu.make_async_copy(first_back_hbm.at[acc], first_back, local_sem.at[5]),
        pltpu.make_async_copy(third_hbm, third, local_sem.at[7]),
        pltpu.make_async_copy(third_back_hbm, third_back, local_sem.at[8]),
        pltpu.make_async_copy(flip_hbm, flip, local_sem.at[9]),
    ]
    own_recip = pltpu.make_async_copy(recip_hbm, recip, local_sem.at[6])
    own_limbs.start()
    own_recip.start()
    for copy in local:
        copy.start()
    own_limbs.wait()

    def clear(mid, carry):
        start = pl.multiple_of(mid * PADDED, PADDED)
        back[pl.ds(start + 16, PADDED - 16)] = jnp.zeros((PADDED - 16, LANES), jnp.float32)
        return carry

    lax.fori_loop(0, MID, clear, 0)
    pl.semaphore_wait(barrier, greeted)
    pl.semaphore_signal(ready, inc=1, device_id=above, device_id_type=pl.DeviceIdType.MESH)

    over = [
        remote(
            own.at[pl.ds(piece * PIECE, PIECE)],
            prior.at[pl.ds(piece * PIECE, PIECE)],
            over_send.at[piece],
            over_recv.at[piece],
            later,
        )
        for piece in range(PIECES)
    ]
    for copy in over:
        copy.start()

    def gather(step, piece, source, owner, device):
        return remote(
            source,
            quarter(owner, piece),
            gather_send.at[step, piece],
            gather_recv.at[step, piece],
            device,
        )

    pieces = range(PIECES)
    to_pair = [
        gather(0, piece, other.at[pl.ds(piece * PIECE, PIECE)], acc, partner) for piece in pieces
    ]
    to_twin = [gather(1, piece, quarter(acc, piece), acc, beside) for piece in pieces]
    passed = [gather(2, piece, quarter(pair, piece), pair, beside) for piece in pieces]

    def start_row(odd_row, row):
        return (row // 4) * 256 + 2 * (row % 4) + odd_row

    own_round = parity * 2 + tail
    own_recip.wait()
    for row in range(8):
        start = own_round * 1024 + core * 512 + start_row(1 - odd, row)
        packed[pl.ds(row, MID, stride=8)] = recip[pl.ds(start, MID, stride=8)]

    def share(step, round_index, device):
        slot = paired.at[round_index, core]
        return remote(
            packed if step == 0 else slot,
            slot,
            share_send.at[step],
            share_recv.at[step],
            device,
        )

    across_round = parity * 2 + 1 - tail
    above_round = (1 - parity) * 2 + tail
    far_round = (1 - parity) * 2 + 1 - tail
    fetched = share(0, own_round, partner)
    own_to_mate = share(1, own_round, mate)
    own_across = share(2, own_round, across)
    own_below = share(3, own_round, below)
    across_to_mate = share(4, across_round, mate)
    across_below = share(5, across_round, below)
    above_to_mate = share(6, above_round, mate)
    far_to_mate = share(7, far_round, mate)
    fetched.start()

    def pass_fetched():
        fetched.wait_recv()
        own_across.start()
        own_to_mate.start()

    late = jnp.logical_and(spot == 0, tail == 0)
    pl.when(late)(pass_fetched)
    sign = (1 - 2 * odd).astype(jnp.float32)
    for piece in pieces:
        rows = pl.ds(piece * PIECE, PIECE)
        over[piece].wait_recv()
        signed = prior[rows] * sign
        other[rows] = own[rows] - signed
        to_pair[piece].start()
        limbs[pl.ds(pl.multiple_of(acc * QUARTER + piece * PIECE, PIECE), PIECE)] = (
            own[rows] + signed
        )
        to_twin[piece].start()
    for piece in pieces:
        to_pair[piece].wait_recv()
        passed[piece].start()
    pl.when(jnp.logical_not(late))(pass_fetched)
    pl.semaphore_wait(ready, 1)
    own_below.start()
    for copy in to_twin + passed:
        copy.wait_recv()
    for copy in local:
        copy.wait()

    lower = lax.broadcasted_iota(jnp.int32, (MID // 2, LANES), 1) < 64

    def first_step(turn, carry):
        values = [limbs[pl.ds(GROUP * turn + side, LIMB_ROWS, stride=MID)] for side in range(GROUP)]
        product = left_product(first[...], jnp.concatenate(values, axis=1))
        for side in range(GROUP):
            start = pl.multiple_of((GROUP * turn + side) * PADDED, PADDED)
            mixed[pl.ds(start, PADDED)] = product[:, side * LANES : (side + 1) * LANES]
        return carry

    lax.fori_loop(0, MID // GROUP, first_step, 0)
    own_across.wait_recv()
    across_below.start()
    across_to_mate.start()
    own_below.wait_recv()
    above_to_mate.start()

    def chunk_of(step, chunk):
        return spectra.at[step, :, pl.ds(chunk * CHUNK, CHUNK)]

    def ring(step, chunk):
        return remote(
            chunk_of(step, chunk),
            chunk_of(step + 1, chunk),
            ring_send.at[step, chunk],
            ring_recv.at[step, chunk],
            onward,
        )

    def leave(step, chunk):
        if vias[step] is None:
            return remote(
                chunk_of(0, chunk),
                chunk_of(step + 1, chunk),
                leave_send.at[chunk],
                ring_recv.at[step, chunk],
                along(to_start[step]),
            )
        return remote(
            chunk_of(0, chunk),
            crossing.at[:, pl.ds(chunk * CHUNK, CHUNK)],
            leave_send.at[chunk],
            cross_recv.at[chunk],
            along(to_via[step]),
        )

    def enter(step, chunk):
        return remote(
            crossing.at[:, pl.ds(chunk * CHUNK, CHUNK)],
            chunk_of(step + 1, chunk),
            enter_send.at[chunk],
            ring_recv.at[step, chunk],
            along(to_start[step]),
        )

    def send_on(step, chunk):
        if crosses:

            @pl.when(jnp.logical_not(makers[0]))
            def _():
                ring(step, chunk).start()

        else:
            ring(step, chunk).start()

    def send_across(chunk):
        if crosses:
            for step in range(ROUNDS - 1):

                @pl.when(makers[step])
                def _():
                    leave(step, chunk).start()

    def help_across(chunk):
        if crosses:
            for step in (0, 2):

                @pl.when(vias[step])
                def _():
                    leave(step, chunk).wait_recv()
                    enter(step, chunk).start()

    def forward(chunk, carry):
        reals, imags = [], []
        for place in range(CHUNK):
            row = chunk * CHUNK + place
            value = jnp.concatenate(
                [
                    mixed[pl.ds(row, MID, stride=PADDED)],
                    mixed[pl.ds(ROWS + row, MID, stride=PADDED)],
                ],
                axis=0,
            )
            product = left_product(second[row], value)
            real, imag = product[:MID], product[MID:]
            turn_real, turn_imag = twiddle[row, 0], twiddle[row, 1]
            reals.append(real * turn_real - imag * turn_imag)
            imags.append(real * turn_imag + imag * turn_real)
        value = jnp.concatenate(
            [jnp.concatenate(reals, axis=0), jnp.concatenate(imags, axis=0)], axis=1
        )
        product = right_product(value, third)
        for place in range(CHUNK):
            rows = product[place * MID : (place + 1) * MID]
            spectra[0, 0, chunk * CHUNK + place] = exchanged(rows[:, :LANES], lower)
            spectra[0, 1, chunk * CHUNK + place] = exchanged(rows[:, LANES:], lower)
        send_across(chunk)
        send_on(0, chunk)
        return carry

    lax.fori_loop(0, CHUNKS, forward, 0)
    across_below.wait_recv()
    far_to_mate.start()
    for copy in (own_to_mate, across_to_mate, above_to_mate, far_to_mate):
        copy.wait_recv()

    def pass_ring(step):
        def body(chunk, carry):
            ring(step, chunk).wait_recv()
            send_on(step + 1, chunk)
            if step == 0:
                help_across(chunk)
            return carry

        lax.fori_loop(0, CHUNKS, body, 0)

    def weigh(step, carry):
        for side in range(2):
            high, low = split(paired[step, side])
            turned = dot(jnp.concatenate([high, low], axis=1), flip[...])
            for group in range(MID):
                flipped[side, pl.ds((MID - 1 - group) * 8, 8)] = turned[group * 8 : group * 8 + 8]
            start = step * 1024 + side * 512
            for row in range(ROWS - 1):
                mine = recip[pl.ds(start + start_row(odd, row), MID, stride=8)]
                mirrored = 7 if row == 0 else 8 - row - odd
                theirs = flipped[side, pl.ds(mirrored, MID, stride=8)]
                if row == 0:
                    theirs = jnp.where(odd == 1, theirs, 0.0)
                weights[step, side, row] = mine + theirs if side == 0 else mine - theirs
            extra = paired[step, side, pl.ds(0, MID, stride=8)]
            weights[step, side, ROWS - 1] = jnp.where(odd == 1, 0.0, extra)
        return carry

    lax.fori_loop(0, ROUNDS, weigh, 0)
    pass_ring(0)
    pass_ring(1)

    def arrive(chunk, carry):
        ring(2, chunk).wait_recv()
        reals, imags = [], []
        for place in range(CHUNK):
            row = chunk * CHUNK + place
            total_real = total_imag = None
            for step in range(ROUNDS):
                weight_real, weight_imag = weights[step, 0, row], weights[step, 1, row]
                real, imag = spectra[step, 0, row], spectra[step, 1, row]
                term_real = weight_real * real - weight_imag * imag
                term_imag = weight_real * imag + weight_imag * real
                total_real = term_real if step == 0 else total_real + term_real
                total_imag = term_imag if step == 0 else total_imag + term_imag
            reals.append(exchanged(total_real, lower))
            imags.append(exchanged(total_imag, lower))
        value = jnp.concatenate(
            [jnp.concatenate(reals, axis=0), jnp.concatenate(imags, axis=0)], axis=1
        )
        product = right_product(value, third_back)
        for place in range(CHUNK):
            row = chunk * CHUNK + place
            real = product[place * MID : (place + 1) * MID, :LANES]
            imag = product[place * MID : (place + 1) * MID, LANES:]
            turn_real, turn_imag = twiddle[row, 0], twiddle[row, 1]
            turned = jnp.concatenate(
                [real * turn_real + imag * turn_imag, imag * turn_real - real * turn_imag], axis=0
            )
            unmixed = left_product(second_back[row], turned)
            back[pl.ds(row, MID, stride=PADDED)] = unmixed[:MID]
            back[pl.ds(ROWS + row, MID, stride=PADDED)] = unmixed[MID:]
        return carry

    lax.fori_loop(0, CHUNKS, arrive, 0)

    def unmix(table, target, count):
        def body(turn, carry):
            values = []
            for side in range(GROUP):
                start = pl.multiple_of((GROUP * turn + side) * PADDED, PADDED)
                values.append(back[pl.ds(start, PADDED)])
            product = left_product(table, jnp.concatenate(values, axis=1))
            for side in range(GROUP):
                target[pl.ds(GROUP * turn + side, count, stride=MID)] = product[
                    :, side * LANES : (side + 1) * LANES
                ]
            return carry

        lax.fori_loop(0, MID // GROUP, body, 0)

    unmix(first_back[:16], opposed, 8)
    def part(place, start):
        return result.at[pl.ds((place - 1) * QUARTER + start, HALF)]

    to_right = remote(opposed.at[pl.ds(0, HALF)], transit.at[0], sum_send.at[0], sum_recv.at[0], right)
    to_left = remote(opposed.at[pl.ds(HALF, HALF)], transit.at[1], sum_send.at[1], sum_recv.at[1], left)
    plain_right = remote(part(1, HALF), arrived.at[0], sum_send.at[2], sum_recv.at[2], right)
    plain_left = remote(part(2, 0), arrived.at[1], sum_send.at[3], sum_recv.at[3], left)
    summed_right = remote(part(1, 0), arrived.at[2], sum_send.at[4], sum_recv.at[4], right)
    summed_left = remote(part(2, HALF), arrived.at[3], sum_send.at[5], sum_recv.at[5], left)
    to_right.start()
    to_left.start()
    unmix(first_back[16:], result, 24)
    plain_right.start()
    plain_left.start()
    to_right.wait_recv()
    result[:HALF] += transit[0]
    summed_right.start()
    to_left.wait_recv()
    result[QUARTER + HALF : 2 * QUARTER] += transit[1]
    summed_left.start()
    out_ref[...] = result[2 * QUARTER :]
    plain_right.wait_recv()
    out_ref[HALF:] += arrived[0]
    plain_left.wait_recv()
    out_ref[:HALF] += arrived[1]
    summed_right.wait_recv()
    more_ref[:HALF] = arrived[2]
    summed_left.wait_recv()
    more_ref[HALF:] = arrived[3]

    sent = [*over, *to_pair, *to_twin, *passed]
    sent += [fetched, own_to_mate, own_across, own_below, across_to_mate, across_below]
    sent += [above_to_mate, far_to_mate]
    sent += [to_right, to_left, plain_right, plain_left, summed_right, summed_left]
    for copy in sent:
        copy.wait_send()

    def drain(chunk, carry):
        if crosses:
            for step in range(ROUNDS - 1):

                @pl.when(makers[step])
                def _():
                    leave(step, chunk).wait_send()

            for step in (0, 2):

                @pl.when(vias[step])
                def _():
                    enter(step, chunk).wait_send()

            @pl.when(jnp.logical_not(makers[0]))
            def _():
                for step in range(ROUNDS - 1):
                    ring(step, chunk).wait_send()

        else:
            for step in range(ROUNDS - 1):
                ring(step, chunk).wait_send()

        return carry

    lax.fori_loop(0, CHUNKS, drain, 0)


def per_device(blocks, reciprocal_spectra, divisor):
    recip = reciprocal_spectra.reshape(ROUNDS, 2, 2, 8, MID, LANES)
    recip = recip.transpose(0, 1, 2, 4, 3, 5).reshape(ROUNDS * 1024, LANES)
    limbs = divisor.reshape(QUARTER, LANES)
    constants = [jnp.asarray(table) for table in tables()]
    first, second, twiddle, third, third_back, second_back, first_back, flip = constants
    anywhere = pl.BlockSpec(memory_space=pl.ANY)
    vmem = pl.BlockSpec(memory_space=pltpu.VMEM)
    kept, added = pl.pallas_call(
        functools.partial(kernel, blocks),
        out_shape=[jax.ShapeDtypeStruct((QUARTER, LANES), jnp.float32)] * 2,
        in_specs=[anywhere] * 10,
        out_specs=[vmem, vmem],
        scratch_shapes=[
            pltpu.VMEM((ROUNDS * 1024, LANES), jnp.float32),
            pltpu.VMEM((ROUNDS, 2, QUARTER, LANES), jnp.float32),
            pltpu.VMEM((QUARTER, LANES), jnp.float32),
            pltpu.VMEM((2, QUARTER, LANES), jnp.float32),
            pltpu.VMEM((ROUNDS, 2, ROWS, MID, LANES), jnp.float32),
            *[pltpu.VMEM((QUARTER, LANES), jnp.float32)] * 3,
            pltpu.VMEM((ACC * QUARTER, LANES), jnp.float32),
            pltpu.VMEM(first.shape[1:], jnp.bfloat16),
            pltpu.VMEM(second.shape[1:], jnp.bfloat16),
            pltpu.VMEM(twiddle.shape[1:], jnp.float32),
            pltpu.VMEM(third.shape, jnp.bfloat16),
            pltpu.VMEM(third_back.shape, jnp.bfloat16),
            pltpu.VMEM(flip.shape, jnp.bfloat16),
            pltpu.VMEM(second_back.shape[1:], jnp.bfloat16),
            pltpu.VMEM(first_back.shape[1:], jnp.bfloat16),
            pltpu.VMEM((MID * PADDED, LANES), jnp.float32),
            pltpu.VMEM((ROUNDS, 2, ROWS, MID, LANES), jnp.float32),
            pltpu.VMEM((2, ROWS, MID, LANES), jnp.float32),
            pltpu.VMEM((MID * PADDED, LANES), jnp.float32),
            pltpu.VMEM(((ACC - 1) * QUARTER, LANES), jnp.float32),
            pltpu.VMEM((QUARTER, LANES), jnp.float32),
            pltpu.VMEM((2, HALF, LANES), jnp.float32),
            pltpu.VMEM((4, HALF, LANES), jnp.float32),
            pltpu.SemaphoreType.DMA((10,)),
            pltpu.SemaphoreType.DMA((PIECES,)),
            pltpu.SemaphoreType.DMA((PIECES,)),
            pltpu.SemaphoreType.DMA((3, PIECES)),
            pltpu.SemaphoreType.DMA((3, PIECES)),
            pltpu.SemaphoreType.DMA((8,)),
            pltpu.SemaphoreType.DMA((8,)),
            pltpu.SemaphoreType.DMA((ROUNDS - 1, CHUNKS)),
            pltpu.SemaphoreType.DMA((ROUNDS - 1, CHUNKS)),
            pltpu.SemaphoreType.DMA((CHUNKS,)),
            pltpu.SemaphoreType.DMA((CHUNKS,)),
            pltpu.SemaphoreType.DMA((CHUNKS,)),
            pltpu.SemaphoreType.DMA((6,)),
            pltpu.SemaphoreType.DMA((6,)),
            pltpu.SemaphoreType.REGULAR,
        ],
        compiler_params=pltpu.CompilerParams(
            collective_id=0, has_side_effects=True, vmem_limit_bytes=60 * 1024 * 1024
        ),
    )(recip, limbs, first, second, twiddle, third, third_back, flip, second_back, first_back)
    return kept.reshape(1, QUARTER * LANES) + added.reshape(1, QUARTER * LANES)


def solution(mesh):
    in_specs = (P(None, None, "acc", None), P(("blk", "tail"), "acc"))
    out_specs = P(("blk", "tail"), "acc")
    return jax.shard_map(
        functools.partial(per_device, mesh.shape["blk"]),
        mesh=mesh,
        in_specs=in_specs,
        out_specs=out_specs,
        check_vma=False,
    )
```

```python
import functools

import jax
import jax.numpy as jnp
import ml_dtypes
import numpy as np
from jax import lax
from jax.experimental import pallas as pl
from jax.experimental.pallas import tpu as pltpu
from jax.sharding import PartitionSpec as P

LENGTH = 262144
ACC = 4
OWNED = 16
ROWS = 9
LIMB_ROWS = 32
PIECES = 2
PIECE = 256 // PIECES
PADDED = 32
OUTER = 64
MID = 32
LANES = 128
QUARTER = 256
HALF = QUARTER // 2
CHUNK = 3
CHUNKS = ROWS // CHUNK
ROUNDS = 4
CORES = 2
GROUP = 32
CYCLE = 16


def high_low(table):
    high = table.astype(ml_dtypes.bfloat16)
    low = (table - high.astype(np.float64)).astype(ml_dtypes.bfloat16)
    return high, low


def stacked_left(table):
    high, low = high_low(table)
    return np.concatenate(
        [
            np.concatenate([high, high], axis=-1),
            np.concatenate([low, np.zeros_like(low)], axis=-1),
        ],
        axis=-2,
    )


def root(product, modulus):
    angle = (product % modulus) * (-2.0 * np.pi / modulus)
    return np.cos(angle), np.sin(angle)


def rows_of(place):
    odd = place // 2
    own = OWNED * place + 2 * np.arange(8) + odd
    return np.append(own, own[0] if odd else OWNED * (ACC - 1 - place))


@functools.lru_cache(maxsize=None)
def tables():
    rows = np.stack([rows_of(place) for place in range(ACC)])
    limb = np.arange(LIMB_ROWS)
    mid = np.arange(MID)
    lane = np.arange(LANES)
    kappa = np.concatenate([np.arange(0, MID, 2), np.arange(1, MID, 2)])
    bins = 2 * (lane % 64) + lane // 64
    first, first_back = [], []
    for place in range(ACC):
        own = rows[place]
        real, imag = root(own[:, None] * limb[None, :], OUTER)
        empty = np.zeros((PADDED - 2 * ROWS, LIMB_ROWS))
        first.append(stacked_left(np.concatenate([real, imag, empty], axis=0)))
        order = [(place + 2) % ACC, (place + 1) % ACC, (place + 3) % ACC, place]
        kept = np.concatenate([np.arange(8 * q, 8 * q + 8) for q in order])
        real, imag = root(kept[:, None] * own[None, :], OUTER)
        empty = np.zeros((len(kept), PADDED - 2 * ROWS))
        table = np.concatenate([real, imag, empty], axis=1) / LENGTH
        first_back.append(
            np.concatenate([stacked_left(table[:8]), stacked_left(table[8:])], axis=0)
        )
    freq = rows[:, :, None] + OUTER * kappa
    real, imag = root(freq[..., None] * mid, 2048)
    second = stacked_left(
        np.concatenate(
            [np.concatenate([real, -imag], axis=-1), np.concatenate([imag, real], axis=-1)], axis=-2
        )
    )
    real, imag = real.swapaxes(-1, -2), -imag.swapaxes(-1, -2)
    second_back = stacked_left(
        np.concatenate(
            [np.concatenate([real, -imag], axis=-1), np.concatenate([imag, real], axis=-1)], axis=-2
        )
    )
    real, imag = root(freq[..., None] * lane, LENGTH)
    twiddle = np.stack([real, imag], axis=2).astype(np.float32)
    real, imag = root(lane[:, None] * bins[None, :], LANES)
    third = np.stack(
        high_low(
            np.concatenate(
                [np.concatenate([real, imag], axis=1), np.concatenate([-imag, real], axis=1)], axis=0
            )
        )
    )
    real, imag = real.T, -imag.T
    third_back = np.stack(
        high_low(
            np.concatenate(
                [np.concatenate([real, imag], axis=1), np.concatenate([-imag, real], axis=1)], axis=0
            )
        )
    )
    return (
        np.stack(first),
        second,
        twiddle,
        third,
        third_back,
        second_back,
        np.stack(first_back),
        np.concatenate([np.eye(LANES)[::-1]] * 2, axis=0).astype(ml_dtypes.bfloat16),
    )


def split(value):
    high = value.astype(jnp.bfloat16)
    low = (value - high.astype(jnp.float32)).astype(jnp.bfloat16)
    return high, low


def dot(first, second):
    return jnp.dot(first, second, preferred_element_type=jnp.float32)


def left_product(stacked, value):
    high, low = split(value)
    both = dot(stacked, jnp.concatenate([high, low], axis=0))
    rows = both.shape[0] // 2
    return both[:rows] + both[rows:]


def right_product(value, table):
    high, low = split(value)
    rows = value.shape[0]
    both = dot(jnp.concatenate([high, low], axis=0), table[0])
    return both[:rows] + both[rows:] + dot(high, table[1])


def exchanged(value, lower):
    top, bottom = value[: MID // 2], value[MID // 2 :]
    return jnp.concatenate(
        [
            jnp.where(lower, top, pltpu.roll(bottom, 64, 1)),
            jnp.where(lower, pltpu.roll(top, 64, 1), bottom),
        ],
        axis=0,
    )


def kernel(
    blocks,
    recip_hbm,
    limbs_hbm,
    first_hbm,
    second_hbm,
    twiddle_hbm,
    third_hbm,
    third_back_hbm,
    flip_hbm,
    second_back_hbm,
    first_back_hbm,
    out_ref,
    more_ref,
    recip,
    paired,
    packed,
    flipped,
    weights,
    own,
    prior,
    other,
    limbs,
    first,
    second,
    twiddle,
    third,
    third_back,
    flip,
    second_back,
    first_back,
    mixed,
    spectra,
    crossing,
    back,
    result,
    opposed,
    transit,
    arrived,
    local_sem,
    over_send,
    over_recv,
    gather_send,
    gather_recv,
    share_send,
    share_recv,
    ring_send,
    ring_recv,
    leave_send,
    enter_send,
    cross_recv,
    sum_send,
    sum_recv,
    ready,
):
    blk = lax.axis_index("blk")
    acc = lax.axis_index("acc")
    tail = lax.axis_index("tail")
    right = {"blk": blk, "acc": lax.rem(acc + 1, ACC), "tail": tail}
    left = {"blk": blk, "acc": lax.rem(acc + ACC - 1, ACC), "tail": tail}
    later = {"blk": lax.rem(blk + tail, blocks), "acc": acc, "tail": 1 - tail}
    earlier = {"blk": lax.rem(blk + blocks - 1 + tail, blocks), "acc": acc, "tail": 1 - tail}
    onward = {"blk": lax.rem(blk + 1, blocks), "acc": acc, "tail": tail}
    backward = {"blk": lax.rem(blk + blocks - 1, blocks), "acc": acc, "tail": tail}
    odd = acc // 2
    pair = ACC - 1 - acc
    twin = acc + 1 - 2 * lax.rem(acc, 2)
    beside = {"blk": blk, "acc": twin, "tail": tail}
    partner = {"blk": blk, "acc": ACC - 1 - acc, "tail": tail}
    cycle = min(CYCLE, blocks)
    spot = lax.rem(blk, cycle)
    core = lax.rem(blk, CORES)
    parity = lax.rem(spot // CORES, 2)
    across = {"blk": blk, "acc": acc, "tail": 1 - tail}
    mate = {"blk": blk + 1 - 2 * core, "acc": acc, "tail": tail}
    below = {"blk": blk - spot + lax.rem(spot + cycle - CORES, cycle), "acc": acc, "tail": tail}
    above = {"blk": blk - spot + lax.rem(spot + CORES, cycle), "acc": acc, "tail": tail}
    crosses = blocks > cycle
    makers = [spot == cycle - 1 - step for step in range(ROUNDS - 1)]
    vias = [spot == 1, None, spot == cycle // 2 - 1]
    to_via = [blocks - cycle + 2, None, cycle // 2 + 2]
    to_start = [cycle - 1, 2, blocks - cycle // 2 + 1]

    def along(steps):
        return {"blk": lax.rem(blk + steps, blocks), "acc": acc, "tail": tail}

    def remote(src, dst, send_sem, recv_sem, device):
        return pltpu.make_async_remote_copy(
            src_ref=src,
            dst_ref=dst,
            send_sem=send_sem,
            recv_sem=recv_sem,
            device_id=device,
            device_id_type=pl.DeviceIdType.MESH,
        )

    def quarter(owner, piece):
        return limbs.at[pl.ds(pl.multiple_of(owner * QUARTER + piece * PIECE, PIECE), PIECE)]

    barrier = pltpu.get_barrier_semaphore()
    for device in (right, left, earlier, backward, mate, across, below):
        pl.semaphore_signal(barrier, inc=1, device_id=device, device_id_type=pl.DeviceIdType.MESH)

    def greet(steps):
        pl.semaphore_signal(
            barrier,
            inc=1,
            device_id=along(blocks - steps),
            device_id_type=pl.DeviceIdType.MESH,
        )

    greeted = 7
    if crosses:
        for place in (*makers, vias[0], vias[2]):
            greeted += jnp.where(place, 1, 0)

        @pl.when(spot == 0)
        def _():
            for steps in to_start:
                greet(steps)

        for step in (0, 2):

            @pl.when(vias[step])
            def _():
                greet(to_via[step])

    own_limbs = pltpu.make_async_copy(limbs_hbm, own, local_sem.at[0])
    local = [
        pltpu.make_async_copy(first_hbm.at[acc], first, local_sem.at[1]),
        pltpu.make_async_copy(second_hbm.at[acc], second, local_sem.at[2]),
        pltpu.make_async_copy(twiddle_hbm.at[acc], twiddle, local_sem.at[3]),
        pltpu.make_async_copy(second_back_hbm.at[acc], second_back, local_sem.at[4]),
        pltpu.make_async_copy(first_back_hbm.at[acc], first_back, local_sem.at[5]),
        pltpu.make_async_copy(third_hbm, third, local_sem.at[7]),
        pltpu.make_async_copy(third_back_hbm, third_back, local_sem.at[8]),
        pltpu.make_async_copy(flip_hbm, flip, local_sem.at[9]),
    ]
    own_recip = pltpu.make_async_copy(recip_hbm, recip, local_sem.at[6])
    own_limbs.start()
    own_recip.start()
    for copy in local:
        copy.start()
    own_limbs.wait()

    def clear(mid, carry):
        start = pl.multiple_of(mid * PADDED, PADDED)
        back[pl.ds(start + 16, PADDED - 16)] = jnp.zeros((PADDED - 16, LANES), jnp.float32)
        return carry

    lax.fori_loop(0, MID, clear, 0)
    pl.semaphore_wait(barrier, greeted)
    pl.semaphore_signal(ready, inc=1, device_id=above, device_id_type=pl.DeviceIdType.MESH)

    over = [
        remote(
            own.at[pl.ds(piece * PIECE, PIECE)],
            prior.at[pl.ds(piece * PIECE, PIECE)],
            over_send.at[piece],
            over_recv.at[piece],
            later,
        )
        for piece in range(PIECES)
    ]
    for copy in over:
        copy.start()

    def gather(step, piece, source, owner, device):
        return remote(
            source,
            quarter(owner, piece),
            gather_send.at[step, piece],
            gather_recv.at[step, piece],
            device,
        )

    pieces = range(PIECES)
    to_pair = [
        gather(0, piece, other.at[pl.ds(piece * PIECE, PIECE)], acc, partner) for piece in pieces
    ]
    to_twin = [gather(1, piece, quarter(acc, piece), acc, beside) for piece in pieces]
    passed = [gather(2, piece, quarter(pair, piece), pair, beside) for piece in pieces]

    def start_row(odd_row, row):
        return (row // 4) * 256 + 2 * (row % 4) + odd_row

    own_round = parity * 2 + tail
    own_recip.wait()
    for row in range(8):
        start = own_round * 1024 + core * 512 + start_row(1 - odd, row)
        packed[pl.ds(row, MID, stride=8)] = recip[pl.ds(start, MID, stride=8)]

    def share(step, round_index, device):
        slot = paired.at[round_index, core]
        return remote(
            packed if step == 0 else slot,
            slot,
            share_send.at[step],
            share_recv.at[step],
            device,
        )

    across_round = parity * 2 + 1 - tail
    above_round = (1 - parity) * 2 + tail
    far_round = (1 - parity) * 2 + 1 - tail
    fetched = share(0, own_round, partner)
    own_to_mate = share(1, own_round, mate)
    own_across = share(2, own_round, across)
    own_below = share(3, own_round, below)
    across_to_mate = share(4, across_round, mate)
    across_below = share(5, across_round, below)
    above_to_mate = share(6, above_round, mate)
    far_to_mate = share(7, far_round, mate)
    fetched.start()

    def pass_fetched():
        fetched.wait_recv()
        own_across.start()
        own_to_mate.start()

    late = jnp.logical_and(spot == 0, tail == 0)
    pl.when(late)(pass_fetched)
    sign = (1 - 2 * odd).astype(jnp.float32)
    for piece in pieces:
        rows = pl.ds(piece * PIECE, PIECE)
        over[piece].wait_recv()
        signed = prior[rows] * sign
        other[rows] = own[rows] - signed
        to_pair[piece].start()
        limbs[pl.ds(pl.multiple_of(acc * QUARTER + piece * PIECE, PIECE), PIECE)] = (
            own[rows] + signed
        )
        to_twin[piece].start()
    for piece in pieces:
        to_pair[piece].wait_recv()
        passed[piece].start()
    pl.when(jnp.logical_not(late))(pass_fetched)
    pl.semaphore_wait(ready, 1)
    own_below.start()
    for copy in to_twin + passed:
        copy.wait_recv()
    for copy in local:
        copy.wait()

    lower = lax.broadcasted_iota(jnp.int32, (MID // 2, LANES), 1) < 64

    def first_step(turn, carry):
        values = [limbs[pl.ds(GROUP * turn + side, LIMB_ROWS, stride=MID)] for side in range(GROUP)]
        product = left_product(first[...], jnp.concatenate(values, axis=1))
        for side in range(GROUP):
            start = pl.multiple_of((GROUP * turn + side) * PADDED, PADDED)
            mixed[pl.ds(start, PADDED)] = product[:, side * LANES : (side + 1) * LANES]
        return carry

    lax.fori_loop(0, MID // GROUP, first_step, 0)
    own_across.wait_recv()
    across_below.start()
    across_to_mate.start()
    own_below.wait_recv()
    above_to_mate.start()

    def chunk_of(step, chunk):
        return spectra.at[step, :, pl.ds(chunk * CHUNK, CHUNK)]

    def ring(step, chunk):
        return remote(
            chunk_of(step, chunk),
            chunk_of(step + 1, chunk),
            ring_send.at[step, chunk],
            ring_recv.at[step, chunk],
            onward,
        )

    def leave(step, chunk):
        if vias[step] is None:
            return remote(
                chunk_of(0, chunk),
                chunk_of(step + 1, chunk),
                leave_send.at[chunk],
                ring_recv.at[step, chunk],
                along(to_start[step]),
            )
        return remote(
            chunk_of(0, chunk),
            crossing.at[:, pl.ds(chunk * CHUNK, CHUNK)],
            leave_send.at[chunk],
            cross_recv.at[chunk],
            along(to_via[step]),
        )

    def enter(step, chunk):
        return remote(
            crossing.at[:, pl.ds(chunk * CHUNK, CHUNK)],
            chunk_of(step + 1, chunk),
            enter_send.at[chunk],
            ring_recv.at[step, chunk],
            along(to_start[step]),
        )

    def send_on(step, chunk):
        if crosses:

            @pl.when(jnp.logical_not(makers[0]))
            def _():
                ring(step, chunk).start()

        else:
            ring(step, chunk).start()

    def send_across(chunk):
        if crosses:
            for step in range(ROUNDS - 1):

                @pl.when(makers[step])
                def _():
                    leave(step, chunk).start()

    def help_across(chunk):
        if crosses:
            for step in (0, 2):

                @pl.when(vias[step])
                def _():
                    leave(step, chunk).wait_recv()
                    enter(step, chunk).start()

    def forward(chunk, carry):
        reals, imags = [], []
        for place in range(CHUNK):
            row = chunk * CHUNK + place
            value = jnp.concatenate(
                [
                    mixed[pl.ds(row, MID, stride=PADDED)],
                    mixed[pl.ds(ROWS + row, MID, stride=PADDED)],
                ],
                axis=0,
            )
            product = left_product(second[row], value)
            real, imag = product[:MID], product[MID:]
            turn_real, turn_imag = twiddle[row, 0], twiddle[row, 1]
            reals.append(real * turn_real - imag * turn_imag)
            imags.append(real * turn_imag + imag * turn_real)
        value = jnp.concatenate(
            [jnp.concatenate(reals, axis=0), jnp.concatenate(imags, axis=0)], axis=1
        )
        product = right_product(value, third)
        for place in range(CHUNK):
            rows = product[place * MID : (place + 1) * MID]
            spectra[0, 0, chunk * CHUNK + place] = exchanged(rows[:, :LANES], lower)
            spectra[0, 1, chunk * CHUNK + place] = exchanged(rows[:, LANES:], lower)
        send_across(chunk)
        send_on(0, chunk)
        return carry

    lax.fori_loop(0, CHUNKS, forward, 0)
    across_below.wait_recv()
    far_to_mate.start()
    for copy in (own_to_mate, across_to_mate, above_to_mate, far_to_mate):
        copy.wait_recv()

    def pass_ring(step):
        def body(chunk, carry):
            ring(step, chunk).wait_recv()
            send_on(step + 1, chunk)
            if step == 0:
                help_across(chunk)
            return carry

        lax.fori_loop(0, CHUNKS, body, 0)

    def weigh(step, carry):
        for side in range(2):
            high, low = split(paired[step, side])
            turned = dot(jnp.concatenate([high, low], axis=1), flip[...])
            for group in range(MID):
                flipped[side, pl.ds((MID - 1 - group) * 8, 8)] = turned[group * 8 : group * 8 + 8]
            start = step * 1024 + side * 512
            for row in range(ROWS - 1):
                mine = recip[pl.ds(start + start_row(odd, row), MID, stride=8)]
                mirrored = 7 if row == 0 else 8 - row - odd
                theirs = flipped[side, pl.ds(mirrored, MID, stride=8)]
                if row == 0:
                    theirs = jnp.where(odd == 1, theirs, 0.0)
                weights[step, side, row] = mine + theirs if side == 0 else mine - theirs
            extra = paired[step, side, pl.ds(0, MID, stride=8)]
            weights[step, side, ROWS - 1] = jnp.where(odd == 1, 0.0, extra)
        return carry

    lax.fori_loop(0, ROUNDS, weigh, 0)
    pass_ring(0)
    pass_ring(1)

    def arrive(chunk, carry):
        ring(2, chunk).wait_recv()
        reals, imags = [], []
        for place in range(CHUNK):
            row = chunk * CHUNK + place
            total_real = total_imag = None
            for step in range(ROUNDS):
                weight_real, weight_imag = weights[step, 0, row], weights[step, 1, row]
                real, imag = spectra[step, 0, row], spectra[step, 1, row]
                term_real = weight_real * real - weight_imag * imag
                term_imag = weight_real * imag + weight_imag * real
                total_real = term_real if step == 0 else total_real + term_real
                total_imag = term_imag if step == 0 else total_imag + term_imag
            reals.append(exchanged(total_real, lower))
            imags.append(exchanged(total_imag, lower))
        value = jnp.concatenate(
            [jnp.concatenate(reals, axis=0), jnp.concatenate(imags, axis=0)], axis=1
        )
        product = right_product(value, third_back)
        for place in range(CHUNK):
            row = chunk * CHUNK + place
            real = product[place * MID : (place + 1) * MID, :LANES]
            imag = product[place * MID : (place + 1) * MID, LANES:]
            turn_real, turn_imag = twiddle[row, 0], twiddle[row, 1]
            turned = jnp.concatenate(
                [real * turn_real + imag * turn_imag, imag * turn_real - real * turn_imag], axis=0
            )
            unmixed = left_product(second_back[row], turned)
            back[pl.ds(row, MID, stride=PADDED)] = unmixed[:MID]
            back[pl.ds(ROWS + row, MID, stride=PADDED)] = unmixed[MID:]
        return carry

    lax.fori_loop(0, CHUNKS, arrive, 0)

    def unmix(table, target, count):
        def body(turn, carry):
            values = []
            for side in range(GROUP):
                start = pl.multiple_of((GROUP * turn + side) * PADDED, PADDED)
                values.append(back[pl.ds(start, PADDED)])
            product = left_product(table, jnp.concatenate(values, axis=1))
            for side in range(GROUP):
                target[pl.ds(GROUP * turn + side, count, stride=MID)] = product[
                    :, side * LANES : (side + 1) * LANES
                ]
            return carry

        lax.fori_loop(0, MID // GROUP, body, 0)

    unmix(first_back[:16], opposed, 8)
    def part(place, start):
        return result.at[pl.ds((place - 1) * QUARTER + start, HALF)]

    to_right = remote(opposed.at[pl.ds(0, HALF)], transit.at[0], sum_send.at[0], sum_recv.at[0], right)
    to_left = remote(opposed.at[pl.ds(HALF, HALF)], transit.at[1], sum_send.at[1], sum_recv.at[1], left)
    plain_right = remote(part(1, HALF), arrived.at[0], sum_send.at[2], sum_recv.at[2], right)
    plain_left = remote(part(2, 0), arrived.at[1], sum_send.at[3], sum_recv.at[3], left)
    summed_right = remote(part(1, 0), arrived.at[2], sum_send.at[4], sum_recv.at[4], right)
    summed_left = remote(part(2, HALF), arrived.at[3], sum_send.at[5], sum_recv.at[5], left)
    to_right.start()
    to_left.start()
    unmix(first_back[16:], result, 24)
    plain_right.start()
    plain_left.start()
    to_right.wait_recv()
    result[:HALF] += transit[0]
    summed_right.start()
    to_left.wait_recv()
    result[QUARTER + HALF : 2 * QUARTER] += transit[1]
    summed_left.start()
    out_ref[...] = result[2 * QUARTER :]
    plain_right.wait_recv()
    out_ref[HALF:] += arrived[0]
    plain_left.wait_recv()
    out_ref[:HALF] += arrived[1]
    summed_right.wait_recv()
    more_ref[:HALF] = arrived[2]
    summed_left.wait_recv()
    more_ref[HALF:] = arrived[3]

    sent = [*over, *to_pair, *to_twin, *passed]
    sent += [fetched, own_to_mate, own_across, own_below, across_to_mate, across_below]
    sent += [above_to_mate, far_to_mate]
    sent += [to_right, to_left, plain_right, plain_left, summed_right, summed_left]
    for copy in sent:
        copy.wait_send()

    def drain(chunk, carry):
        if crosses:
            for step in range(ROUNDS - 1):

                @pl.when(makers[step])
                def _():
                    leave(step, chunk).wait_send()

            for step in (0, 2):

                @pl.when(vias[step])
                def _():
                    enter(step, chunk).wait_send()

            @pl.when(jnp.logical_not(makers[0]))
            def _():
                for step in range(ROUNDS - 1):
                    ring(step, chunk).wait_send()

        else:
            for step in range(ROUNDS - 1):
                ring(step, chunk).wait_send()

        return carry

    lax.fori_loop(0, CHUNKS, drain, 0)


def per_device(blocks, reciprocal_spectra, divisor):
    recip = reciprocal_spectra.reshape(ROUNDS, 2, 2, 8, MID, LANES)
    recip = recip.transpose(0, 1, 2, 4, 3, 5).reshape(ROUNDS * 1024, LANES)
    limbs = divisor.reshape(QUARTER, LANES)
    constants = [jnp.asarray(table) for table in tables()]
    first, second, twiddle, third, third_back, second_back, first_back, flip = constants
    anywhere = pl.BlockSpec(memory_space=pl.ANY)
    vmem = pl.BlockSpec(memory_space=pltpu.VMEM)
    kept, added = pl.pallas_call(
        functools.partial(kernel, blocks),
        out_shape=[jax.ShapeDtypeStruct((QUARTER, LANES), jnp.float32)] * 2,
        in_specs=[anywhere] * 10,
        out_specs=[vmem, vmem],
        scratch_shapes=[
            pltpu.VMEM((ROUNDS * 1024, LANES), jnp.float32),
            pltpu.VMEM((ROUNDS, 2, QUARTER, LANES), jnp.float32),
            pltpu.VMEM((QUARTER, LANES), jnp.float32),
            pltpu.VMEM((2, QUARTER, LANES), jnp.float32),
            pltpu.VMEM((ROUNDS, 2, ROWS, MID, LANES), jnp.float32),
            *[pltpu.VMEM((QUARTER, LANES), jnp.float32)] * 3,
            pltpu.VMEM((ACC * QUARTER, LANES), jnp.float32),
            pltpu.VMEM(first.shape[1:], jnp.bfloat16),
            pltpu.VMEM(second.shape[1:], jnp.bfloat16),
            pltpu.VMEM(twiddle.shape[1:], jnp.float32),
            pltpu.VMEM(third.shape, jnp.bfloat16),
            pltpu.VMEM(third_back.shape, jnp.bfloat16),
            pltpu.VMEM(flip.shape, jnp.bfloat16),
            pltpu.VMEM(second_back.shape[1:], jnp.bfloat16),
            pltpu.VMEM(first_back.shape[1:], jnp.bfloat16),
            pltpu.VMEM((MID * PADDED, LANES), jnp.float32),
            pltpu.VMEM((ROUNDS, 2, ROWS, MID, LANES), jnp.float32),
            pltpu.VMEM((2, ROWS, MID, LANES), jnp.float32),
            pltpu.VMEM((MID * PADDED, LANES), jnp.float32),
            pltpu.VMEM(((ACC - 1) * QUARTER, LANES), jnp.float32),
            pltpu.VMEM((QUARTER, LANES), jnp.float32),
            pltpu.VMEM((2, HALF, LANES), jnp.float32),
            pltpu.VMEM((4, HALF, LANES), jnp.float32),
            pltpu.SemaphoreType.DMA((10,)),
            pltpu.SemaphoreType.DMA((PIECES,)),
            pltpu.SemaphoreType.DMA((PIECES,)),
            pltpu.SemaphoreType.DMA((3, PIECES)),
            pltpu.SemaphoreType.DMA((3, PIECES)),
            pltpu.SemaphoreType.DMA((8,)),
            pltpu.SemaphoreType.DMA((8,)),
            pltpu.SemaphoreType.DMA((ROUNDS - 1, CHUNKS)),
            pltpu.SemaphoreType.DMA((ROUNDS - 1, CHUNKS)),
            pltpu.SemaphoreType.DMA((CHUNKS,)),
            pltpu.SemaphoreType.DMA((CHUNKS,)),
            pltpu.SemaphoreType.DMA((CHUNKS,)),
            pltpu.SemaphoreType.DMA((6,)),
            pltpu.SemaphoreType.DMA((6,)),
            pltpu.SemaphoreType.REGULAR,
        ],
        compiler_params=pltpu.CompilerParams(
            collective_id=0, has_side_effects=True, vmem_limit_bytes=60 * 1024 * 1024
        ),
    )(recip, limbs, first, second, twiddle, third, third_back, flip, second_back, first_back)
    return kept.reshape(1, QUARTER * LANES) + added.reshape(1, QUARTER * LANES)


def solution(mesh):
    in_specs = (P(None, None, "acc", None), P(("blk", "tail"), "acc"))
    out_specs = P(("blk", "tail"), "acc")
    return jax.shard_map(
        functools.partial(per_device, mesh.shape["blk"]),
        mesh=mesh,
        in_specs=in_specs,
        out_specs=out_specs,
        check_vma=False,
    )
```
